32 devices in a mesh: elem: 8 (over z, y), blk: 4 (over x, core).
Axes of the slice: x: 2, y: 2, z: 4, core: 2. Of those that a mesh axis runs over, the one named last changes fastest.
Arguments:
- tangent_in: float32 [4, 64, 16384], P(None, None, ('elem', 'blk')), may hold values from -6 to 6
- forward_state: float32 [4, 64, 16384], P(None, None, ('elem', 'blk')), may hold values from -6 to 6
- adjoint_in: float32 [4, 64, 16384], P(None, None, ('elem', 'blk')), may hold values from -6 to 6
- bulk_modulus: float32 [16384], P(('elem', 'blk')), may hold values from 0.5 to 2
- param_step: float32 [4096], P(('elem', 'blk')), may hold values from -6 to 6
- neighbours: int32 [6, 16384], P(None, ('elem', 'blk')), may hold values from 0 to 767, as said below
- export_slots: int32 [2, 8192], P(None, ('elem', 'blk')), may hold values from 0 to 511, as said below
- param_map: int32 [4096], P(('elem', 'blk')), may hold values from 0 to 4095, as said below
Outputs:
- tangent_out: float32 [4, 64, 16384], P(None, None, ('elem', 'blk'))
- adjoint_out: float32 [4, 64, 16384], P(None, None, ('elem', 'blk'))
- hvp: float32 [4096], P(('elem', 'blk'))
The draws below stay inside these ranges and needn't reach their ends.
Inputs may be any that keep to these rules, and one draw needn't show every extreme that they name: Each device's elements form a slab of 16 x 16 x 2 hexahedra of a periodic box, stored in a permuted order; the slabs are stacked along z in the order of elem+blk. Entries at or above 512 occur only for the faces -z and +z and name ghost slot entry - 512; face neighbours are mutual. `export_slots`: row 0 lists the elements whose +z face borders the next device, row 1 those whose -z face borders the previous device, in the ghost slot order that the receiving device's neighbours use. `param_map`: the block of device d names a parameter cell owned by a device whose index along elem+blk differs from d by at most 2, cyclically; a device owns cells d * 128 to (d + 1) * 128 - 1; every device has blocks whose owner lies exactly 2 below and exactly 2 above.
All inputs are finite; a program needn't handle non-finite values.
Results may differ from the reference program's by a relative error of at most 0.0001.
Values sent between devices are 32-bit elements; how exact they have to be, the bound alone decides.
A program may use at most 64 MiB of HBM per device.

```python
import math
import jax
import jax.numpy as jnp
import numpy as np
from jax import lax

FIELDS = 4
NODES = 64
EX = 16
EY = 16
EZ = 2
BLOCK = 4
REACH = 2
ELEM_DEV = 512
LAYER = 256
PAR_DEV = 128
ELEMENTS = 16384
NPARAM = 4096
N_ELEM = 8
N_BLK = 4


def slot_layout(key):
    devices = N_ELEM * N_BLK
    cells = EX * EY * EZ

    def one_device(index):
        return jax.random.permutation(jax.random.fold_in(key, index), cells).astype(jnp.int32)
    slot_cell = jax.vmap(one_device)(jnp.arange(devices, dtype=jnp.int32))
    cell_slot = jnp.argsort(slot_cell, axis=1).astype(jnp.int32)
    return (slot_cell, cell_slot)


def draw_neighbours(key, part):
    slot_cell, cell_slot = slot_layout(key)
    layer = EX * EY
    x_pos = slot_cell % EX
    y_pos = slot_cell // EX % EY
    z_pos = slot_cell // layer

    def slot_of(x_val, y_val, z_val):
        return jnp.take_along_axis(cell_slot, x_val + EX * y_val + layer * z_val, axis=1)
    ghost = ELEM_DEV + x_pos + EX * y_pos
    faces = [slot_of((x_pos - 1) % EX, y_pos, z_pos), slot_of((x_pos + 1) % EX, y_pos, z_pos), slot_of(x_pos, (y_pos - 1) % EY, z_pos), slot_of(x_pos, (y_pos + 1) % EY, z_pos), jnp.where(z_pos == 0, ghost, slot_of(x_pos, y_pos, jnp.maximum(z_pos - 1, 0))), jnp.where(z_pos == EZ - 1, ghost, slot_of(x_pos, y_pos, jnp.minimum(z_pos + 1, EZ - 1)))]
    return jnp.stack(faces).reshape(6, -1).astype(jnp.int32)


def draw_export_slots(key, part):
    slot_cell, cell_slot = slot_layout(key)
    layer = EX * EY
    rising = cell_slot[:, layer * (EZ - 1):]
    falling = cell_slot[:, :layer]
    return jnp.stack([rising, falling]).reshape(2, -1).astype(jnp.int32)


def draw_param_map(key, part):
    key = jax.random.fold_in(key, 7)
    devices = N_ELEM * N_BLK
    blocks = ELEM_DEV // BLOCK
    key_one, key_two, key_three, key_four = jax.random.split(key, 4)
    offsets = jax.random.randint(key_one, (devices, blocks), -REACH, REACH + 1)
    lowest = jax.random.randint(key_two, (devices, 1), 0, blocks // 2)
    highest = blocks // 2 + jax.random.randint(key_three, (devices, 1), 0, blocks // 2)
    column = jnp.arange(blocks, dtype=jnp.int32)[None, :]
    offsets = jnp.where(column == lowest, -REACH, offsets)
    offsets = jnp.where(column == highest, REACH, offsets)
    owner_dev = (jnp.arange(devices, dtype=jnp.int32)[:, None] + offsets) % devices
    cell_index = jax.random.randint(key_four, (devices, blocks), 0, PAR_DEV)
    cell_index = jnp.where(column == lowest, 0, cell_index)
    cell_index = jnp.where(column == highest, PAR_DEV - 1, cell_index)
    return (owner_dev * PAR_DEV + cell_index).reshape(-1).astype(jnp.int32)


def block_scale(own_key, dims, shards, low, top_value):
    factor_of = 1.0
    for axis_at, shards_of in shards:
        draws = jax.random.uniform(jax.random.fold_in(jax.random.fold_in(own_key, 6), axis_at), (shards_of,), jnp.float32, low / len(shards), top_value / len(shards))
        factor_of = factor_of * jnp.repeat(jnp.exp(draws), dims[axis_at] // shards_of).reshape((-1,) + (1,) * (len(dims) - 1 - axis_at))
    return factor_of


def gaussian(rng, shape, width, most, shards=(), kind=jnp.bfloat16):
    drawn = width * jax.random.normal(rng, shape, jnp.float32)
    if shards:
        drawn = drawn * block_scale(rng, shape, shards, -0.22, 0.18)
    return jnp.clip(drawn, -most, most).astype(kind)


def setup_inputs(seed: int = 0) -> dict:
    arg_keys = jax.random.split(jax.random.key(seed), 9)
    tangent_in = gaussian(arg_keys[0], (FIELDS, NODES, ELEMENTS), 1.0, 6.0, ((2, 32),), jnp.float32)
    forward_state = gaussian(arg_keys[1], (FIELDS, NODES, ELEMENTS), 1.0, 6.0, ((2, 32),), jnp.float32)
    adjoint_in = gaussian(arg_keys[2], (FIELDS, NODES, ELEMENTS), 1.0, 6.0, ((2, 32),), jnp.float32)
    bulk_modulus = jnp.clip(jnp.exp(math.log(2.0) - 1.3862944 * jax.random.uniform(arg_keys[3], (ELEMENTS,), jnp.float32) ** block_scale(arg_keys[3], (ELEMENTS,), ((0, 32),), -0.2, 0.2)), 0.5, 2.0)
    param_step = gaussian(arg_keys[4], (NPARAM,), 1.0, 6.0, ((0, 32),), jnp.float32)
    neighbours = draw_neighbours(jax.random.fold_in(arg_keys[8], 71), 0)
    export_slots = draw_export_slots(jax.random.fold_in(arg_keys[8], 71), 0)
    param_map = draw_param_map(jax.random.fold_in(arg_keys[8], 71), 0)
    return dict(tangent_in=tangent_in, forward_state=forward_state, adjoint_in=adjoint_in, bulk_modulus=bulk_modulus, param_step=param_step, neighbours=neighbours, export_slots=export_slots, param_map=param_map)


ALPHA = 1.0
LIFT = 6.0
DT = 0.1

def derivative_tables():
    points = np.array([-1.0, -1.0 / np.sqrt(5.0), 1.0 / np.sqrt(5.0), 1.0])
    deriv_one = np.zeros((4, 4))
    for row_at in range(4):
        for col_at in range(4):
            if row_at != col_at:
                numerator = np.prod([points[row_at] - points[node_k] for node_k in range(4) if node_k != row_at and node_k != col_at])
                denominator = np.prod([points[col_at] - points[node_k] for node_k in range(4) if node_k != col_at])
                deriv_one[row_at, col_at] = numerator / denominator
        deriv_one[row_at, row_at] = np.sum([1.0 / (points[row_at] - points[node_k]) for node_k in range(4) if node_k != row_at])
    identity_four = np.eye(4)
    deriv_x = np.kron(np.eye(16), deriv_one)
    deriv_y = np.kron(identity_four, np.kron(deriv_one, identity_four))
    deriv_z = np.kron(deriv_one, np.eye(16))
    weights = np.array([1.0 / 6.0, 5.0 / 6.0, 5.0 / 6.0, 1.0 / 6.0])
    mass_weights = np.kron(weights, np.kron(weights, weights))
    stacked = jnp.asarray(np.concatenate([deriv_x, deriv_y, deriv_z], 0), dtype=jnp.float32)
    joined = jnp.asarray(np.concatenate([deriv_x, deriv_y, deriv_z], 1), dtype=jnp.float32)
    return (stacked, joined, jnp.asarray(mass_weights, dtype=jnp.float32))

def face_trace(field_set, face_id):
    fields, elements = (field_set.shape[0], field_set.shape[-1])
    nodes_cube = field_set.reshape(fields, 4, 4, 4, elements)
    end_index = 3 * (face_id % 2)
    face_axis = face_id // 2
    if face_axis == 0:
        face_plane = nodes_cube[:, :, :, end_index, :]
    elif face_axis == 1:
        face_plane = nodes_cube[:, :, end_index, :, :]
    else:
        face_plane = nodes_cube[:, end_index, :, :, :]
    return face_plane.reshape(fields, 16, elements)

def face_add(field_set, face_id, term):
    fields, elements = (field_set.shape[0], field_set.shape[-1])
    nodes_cube = field_set.reshape(fields, 4, 4, 4, elements)
    term_cube = term.reshape(fields, 4, 4, elements)
    end_index = 3 * (face_id % 2)
    face_axis = face_id // 2
    if face_axis == 0:
        nodes_cube = nodes_cube.at[:, :, :, end_index, :].add(term_cube)
    elif face_axis == 1:
        nodes_cube = nodes_cube.at[:, :, end_index, :, :].add(term_cube)
    else:
        nodes_cube = nodes_cube.at[:, end_index, :, :, :].add(term_cube)
    return nodes_cube.reshape(fields, 64, elements)

def operator(field_set, outside, bulk, stacked, joined):
    elements = field_set.shape[-1]
    gradient = jnp.dot(stacked, field_set[0], precision=lax.Precision.HIGHEST).reshape(3, 64, elements)
    divergence = jnp.dot(joined, field_set[1:].reshape(192, elements), precision=lax.Precision.HIGHEST)
    result = jnp.concatenate([(-bulk * divergence)[None], -gradient], 0)
    for face_id in range(6):
        jump_val = outside[face_id] - face_trace(field_set, face_id)
        face_axis = face_id // 2
        face_sign = 2.0 * (face_id % 2) - 1.0
        pressure = LIFT * (0.5 * ALPHA * jump_val[0] - 0.5 * face_sign * bulk * jump_val[1 + face_axis])
        velocity = 0.5 * LIFT * ALPHA * jump_val[1:]
        velocity = velocity.at[face_axis].add(-0.5 * LIFT * face_sign * jump_val[0])
        result = face_add(result, face_id, jnp.concatenate([pressure[None], velocity], 0))
    return result

def sensitivity(field_set, outside, joined):
    elements = field_set.shape[-1]
    divergence = jnp.dot(joined, field_set[1:].reshape(192, elements), precision=lax.Precision.HIGHEST)
    result = (-divergence)[None]
    for face_id in range(6):
        face_axis = face_id // 2
        face_sign = 2.0 * (face_id % 2) - 1.0
        jump_val = outside[face_id][1 + face_axis] - face_trace(field_set, face_id)[1 + face_axis]
        result = face_add(result, face_id, (-0.5 * LIFT * face_sign * jump_val)[None])
    return result[0]

def reference(tangent_in, forward_state, adjoint_in, bulk_modulus, param_step, neighbours, export_slots, param_map):
    stacked, joined, mass_weights = derivative_tables()
    devices = N_ELEM * N_BLK
    local_index = neighbours.reshape(6, devices, ELEM_DEV)
    base_index = (jnp.arange(devices, dtype=jnp.int32) * ELEM_DEV)[:, None]
    rise_rows = jnp.roll(export_slots[0].reshape(devices, LAYER), 1, axis=0)
    fall_rows = jnp.roll(export_slots[1].reshape(devices, LAYER), -1, axis=0)
    ghost_slot = jnp.clip(local_index - ELEM_DEV, 0, LAYER - 1).astype(jnp.int32)
    global_index = []
    for face_id in range(6):
        own_part = base_index + local_index[face_id]
        if face_id == 4:
            remote = jnp.roll(base_index, 1, axis=0) + jnp.take_along_axis(rise_rows, ghost_slot[4], axis=1)
            own_part = jnp.where(local_index[4] < ELEM_DEV, own_part, remote)
        if face_id == 5:
            remote = jnp.roll(base_index, -1, axis=0) + jnp.take_along_axis(fall_rows, ghost_slot[5], axis=1)
            own_part = jnp.where(local_index[5] < ELEM_DEV, own_part, remote)
        global_index.append(own_part.reshape(-1).astype(jnp.int32))

    def outside_of(field_set):
        return [jnp.take(face_trace(field_set, face_id ^ 1), global_index[face_id], axis=2) for face_id in range(6)]

    def linear_map(field_set):
        return operator(field_set, outside_of(field_set), bulk_modulus, stacked, joined)
    sense = sensitivity(forward_state, outside_of(forward_state), joined)
    element_step = jnp.repeat(jnp.take(param_step, param_map), BLOCK)
    change = linear_map(tangent_in)
    change = change.at[0].add(2.0 * bulk_modulus * element_step * sense)
    tangent_out = tangent_in + DT * change
    adjoint = adjoint_in + tangent_out
    unused_value, pullback = jax.vjp(linear_map, adjoint)
    adjoint_out = adjoint + DT * pullback(adjoint)[0]
    element_term = 2.0 * DT * bulk_modulus * lax.optimization_barrier(jnp.sum(mass_weights[:, None] * adjoint[0] * sense, axis=0))
    block_term = element_term.reshape(-1, BLOCK).sum(axis=1)
    hvp = jax.ops.segment_sum(block_term, param_map, num_segments=NPARAM)
    return (tangent_out, adjoint_out, hvp)
```

```python
import functools

import jax
import jax.numpy as jnp
import ml_dtypes
import numpy as np
from jax import lax
from jax.experimental import pallas as pl
from jax.experimental.pallas import tpu as pltpu
from jax.sharding import PartitionSpec as P

BLOCK = 4
REACH = 2
LIFT = 6.0
DT = 0.1
HALF = 0.5 * LIFT
MESH = pl.DeviceIdType.MESH
BF16 = jnp.bfloat16
F32 = jnp.float32


def split_np(matrix):
    high = matrix.astype(np.float32).astype(ml_dtypes.bfloat16)
    low = (matrix - high.astype(np.float64)).astype(np.float32).astype(ml_dtypes.bfloat16)
    return high, low


def tables():
    points = np.array([-1.0, -1.0 / np.sqrt(5.0), 1.0 / np.sqrt(5.0), 1.0])
    one = np.zeros((4, 4))
    for i in range(4):
        for j in range(4):
            if i != j:
                top = np.prod([points[i] - points[k] for k in range(4) if k != i and k != j])
                one[i, j] = top / np.prod([points[j] - points[k] for k in range(4) if k != j])
        one[i, i] = np.sum([1.0 / (points[i] - points[k]) for k in range(4) if k != i])
    eye = np.eye(4)
    deriv = [
        np.kron(np.eye(16), one),
        np.kron(eye, np.kron(one, eye)),
        np.kron(one, np.eye(16)),
    ]
    node = np.arange(64)
    place = [node % 4, node // 4 % 4, node // 16]
    faces = [np.flatnonzero(place[f // 2] == 3 * (f % 2)) for f in range(6)]
    sel = np.zeros((6, 16, 64))
    for f in range(6):
        sel[f, np.arange(16), faces[f]] = 1.0
    count = sel.sum((0, 1))
    local = []
    for d in range(3):
        ends = np.diag(sel[2 * d + 1].sum(0) - sel[2 * d].sum(0))
        local.append(-deriv[d] + HALF * ends)
    weights = np.array([1.0 / 6.0, 5.0 / 6.0, 5.0 / 6.0, 1.0 / 6.0])
    mass = np.kron(weights, np.kron(weights, weights))

    own = np.zeros((256, 256))
    for d in range(3):
        rows = slice(64 + 64 * d, 128 + 64 * d)
        own[:64, rows] = local[d]
        own[rows, :64] = local[d]
    sens = np.concatenate(local, 1)

    sel_t = np.zeros((256, 256))
    sel_f = np.zeros((64, 128))
    sel_a = np.zeros((320, 320))
    lift_t = np.zeros((320, 256))
    lift_s = np.zeros((64, 64))
    lift_a = np.zeros((256, 320))
    for f in range(4):
        d = f // 2
        s = 2.0 * (f % 2) - 1.0
        far = sel[f ^ 1]
        near = sel[f].T
        for k in range(4):
            sel_t[64 * f + 16 * k : 64 * f + 16 * k + 16, 64 * k : 64 * k + 64] = far
        for k in range(5):
            sel_a[80 * f + 16 * k : 80 * f + 16 * k + 16, 64 * k : 64 * k + 64] = far
        sel_f[16 * f : 16 * f + 16, 64 * d : 64 * d + 64] = far
        lift_s[:, 16 * f : 16 * f + 16] = -HALF * s * near
        at = 64 * f
        lift_t[0:64, at : at + 16] += HALF * near
        lift_t[64:128, at + 16 + 16 * d : at + 32 + 16 * d] += -HALF * s * near
        for k in range(3):
            lift_t[128 + 64 * k : 192 + 64 * k, at + 16 + 16 * k : at + 32 + 16 * k] += HALF * near
        lift_t[128 + 64 * d : 192 + 64 * d, at : at + 16] += -HALF * s * near
        at = 80 * f
        lift_a[0:64, at + 64 : at + 80] += HALF * near
        lift_a[0:64, at + 16 + 16 * d : at + 32 + 16 * d] += HALF * s * near
        for k in range(3):
            lift_a[64 + 64 * k : 128 + 64 * k, at + 16 + 16 * k : at + 32 + 16 * k] += HALF * near
        lift_a[64 + 64 * d : 128 + 64 * d, at : at + 16] += HALF * s * near

    own_h, own_l = split_np(own)
    adj_h, adj_l = split_np(own.T)
    sen_h, sen_l = split_np(sens)
    wide = np.zeros((320, 256), own_h.dtype)
    wide[64:] = own_h
    lift_t = lift_t.astype(own_h.dtype)
    lift_s = lift_s.astype(own_h.dtype)
    lift_a = lift_a.astype(own_h.dtype)
    return [
        np.concatenate([wide, wide, lift_t, lift_t], 1),
        own_l,
        np.concatenate([sen_h, sen_h, lift_s, lift_s], 1),
        sen_l,
        np.concatenate([adj_h, adj_h, lift_a, lift_a], 1),
        adj_l,
        sel_t.astype(own_h.dtype),
        sel_f.astype(own_h.dtype),
        sel_a.astype(own_h.dtype),
        np.repeat((DT * HALF * count)[:, None], 128, 1).astype(np.float32),
        np.repeat((2.0 * DT * mass)[:, None], 128, 1).astype(np.float32),
    ]


def dot(a, b):
    return jnp.dot(a, b, preferred_element_type=F32)


def dot_nt(a, b):
    return lax.dot_general(a, b, (((1,), (1,)), ((), ())), preferred_element_type=F32)


def split(value):
    high = value.astype(BF16)
    return high, (value - high.astype(F32)).astype(BF16)


def stack(value):
    return jnp.concatenate(split(value), 0)


def hot(row, rows, base=0):
    width = row.shape[1]
    at = lax.broadcasted_iota(jnp.int32, (rows, width), 0) + base
    return jnp.where(at == row, 1.0, 0.0).astype(BF16)


def wide(column):
    return jnp.concatenate([column] * 4, 1)


def kernel(
    devices,
    n_blk,
    q_ref,
    f_ref,
    a_ref,
    k_ref,
    ps_ref,
    nb_ref,
    ex_ref,
    pm_ref,
    main_m,
    main_l,
    sens_m,
    sens_l,
    adj_m,
    adj_l,
    sel_t,
    sel_f,
    sel_a,
    count_ref,
    mass_ref,
    t_out,
    a_out,
    h_out,
    hots,
    ghots,
    exps,
    x1,
    xs,
    x2,
    wz,
    send1,
    recv1,
    send2,
    recv2,
    table,
    psend,
    hsend,
    hrecv,
    ssem1,
    rsem1,
    ssem2,
    rsem2,
    pssem,
    prsem,
    hssem,
    hrsem,
):
    me = lax.axis_index("elem") * n_blk + lax.axis_index("blk")

    def device(step):
        other = lax.rem(me + step + devices, devices)
        return (other // n_blk, lax.rem(other, n_blk))

    steps = [s for s in range(-REACH, REACH + 1) if s]
    barrier = pltpu.get_barrier_semaphore()
    for s in steps:
        pl.semaphore_signal(barrier, inc=1, device_id=device(s), device_id_type=MESH)

    def remote(src, dst, ssem, rsem, step):
        return pltpu.make_async_remote_copy(
            src_ref=src,
            dst_ref=dst,
            send_sem=ssem,
            recv_sem=rsem,
            device_id=device(step),
            device_id_type=MESH,
        )

    def z_trace(refs, top):
        at = 48 if top else 0
        return jnp.concatenate([r[o + at : o + at + 16, :] for r, o in refs], 0)

    fields = [(q_ref, 0), (q_ref, 64), (q_ref, 128), (q_ref, 192), (f_ref, 192)]
    exports = []
    psend[...] = jnp.broadcast_to(ps_ref[...], psend.shape)
    for way in range(2):
        exps[way] = hot(ex_ref[way : way + 1, :], 512)
        both = stack(z_trace(fields, way == 0))
        x2[way * 160 : way * 160 + 160, :] = both
        gathered = dot(both, exps[way])
        send1[way] = gathered[:80] + gathered[80:]
    pl.semaphore_wait(barrier, len(steps))
    copies1 = []
    for way in range(2):
        copy = remote(send1.at[way], recv1.at[way], ssem1.at[way], rsem1.at[way], 1 - 2 * way)
        copy.start()
        copies1.append(copy)
    pcopies = []
    for i, s in enumerate(steps):
        copy = remote(psend, table.at[REACH - s], pssem.at[i], prsem.at[REACH - s], s)
        copy.start()
        pcopies.append(copy)

    for f in range(6):
        hots[f] = hot(nb_ref[f : f + 1, :], 512)
    for way in range(2):
        ghots[way] = hot(nb_ref[4 + way : 5 + way, :], 256, 512)
    q_h, q_l = split(q_ref[...])
    x1[0:256, :] = q_h
    x1[256:512, :] = q_l
    u_h, u_l = split(f_ref[64:256, :])
    xs[0:192, :] = u_h
    xs[192:384, :] = u_l
    for way in range(2):
        inside = dot(x2[way * 160 : way * 160 + 160, :], hots[4 + way])
        wz[way] = inside[:80] + inside[80:]
    t_h = dot(sel_t[...], x1[0:256, :]).astype(BF16)
    t_l = dot(sel_t[...], x1[256:512, :]).astype(BF16)
    tf_h = dot(sel_f[...], xs[0:128, :]).astype(BF16)
    tf_l = dot(sel_f[...], xs[192:320, :]).astype(BF16)
    for f in range(4):
        big = slice(64 * f, 64 * f + 64)
        small = slice(16 * f, 16 * f + 16)
        lhs = jnp.concatenate([t_h[big], t_l[big], tf_h[small], tf_l[small]], 0)
        far = dot(lhs, hots[f]).astype(BF16)
        x1[512 + 64 * f : 576 + 64 * f, :] = far[0:64]
        x1[768 + 64 * f : 832 + 64 * f, :] = far[64:128]
        xs[384 + 16 * f : 400 + 16 * f, :] = far[128:144]
        xs[448 + 16 * f : 464 + 16 * f, :] = far[144:160]
    main = dot(main_m[...], x1[...])
    main_low = dot(main_l[...], x1[0:256, :])
    sense = dot(sens_m[...], xs[...]) + dot(sens_l[...], xs[0:192, :])
    bulk = jnp.broadcast_to(k_ref[...], (64, 512))

    pm = pm_ref[...]
    cells = ps_ref.shape[1]
    owner = pm // cells
    cell = pm - owner * cells
    where = owner - me + REACH
    where = jnp.where(where < 0, where + devices, where)
    where = jnp.where(where >= devices, where - devices, where)
    cell_hot = hot(cell, cells)
    blocks = pm.shape[1]
    repeat = jnp.where(
        lax.broadcasted_iota(jnp.int32, (blocks, 512), 1) // BLOCK
        == lax.broadcasted_iota(jnp.int32, (blocks, 512), 0),
        1.0,
        0.0,
    ).astype(BF16)
    for copy in pcopies:
        copy.wait()
    table[REACH] = psend[...]
    span = 2 * REACH + 1
    picked = dot(stack(table[...].reshape(8 * span, cells)), cell_hot)
    picked = picked[: 8 * span] + picked[8 * span :]
    block_step = jnp.zeros((8, blocks), F32)
    for o in range(span):
        block_step = jnp.where(where == o, picked[8 * o : 8 * o + 8], block_step)
    spread = dot(stack(block_step), repeat)
    step = jnp.concatenate([spread[:8] + spread[8:]] * 8, 0)

    for way in range(2):
        copies1[way].wait()
        outside = dot(stack(recv1[way]), ghots[way])
        wz[way] = wz[way] + outside[:80] + outside[80:]

    low, high = wz[0], wz[1]

    def z_add(value, first, last):
        return jnp.concatenate([value[0:16] + first, value[16:48], value[48:64] + last], 0)

    sense = z_add(sense, HALF * low[64:80], -HALF * high[64:80])
    r_a = z_add(main[0:64], HALF * low[0:16], HALF * high[0:16])
    r_b = z_add(main[64:128] + main_low[0:64], HALF * low[48:64], -HALF * high[48:64])
    r_b = r_b + 2.0 * step * sense
    count = wide(count_ref[...])
    q = q_ref[0:64, :]
    new = q - count * q + DT * (r_a + bulk * r_b)
    t_out[0:64, :] = new
    lam = a_ref[0:64, :] + new
    lam_p = lam
    k_lam = bulk * lam
    a_out[0:64, :] = lam
    k_h, k_l = split(k_lam)
    p_h, p_l = split(lam)
    x2[0:64, :] = k_h
    x2[320:384, :] = k_l
    x2[256:320, :] = p_h
    x2[576:640, :] = p_l
    ztop = [k_lam[48:64]]
    zbot = [k_lam[0:16]]
    for k in range(3):
        at = 64 + 64 * k
        first, last = low[16 + 16 * k : 32 + 16 * k], high[16 + 16 * k : 32 + 16 * k]
        if k == 2:
            first = first + low[0:16]
            last = last - high[0:16]
        r_u = z_add(main[64 + at : 128 + at] + main_low[at : at + 64], HALF * first, HALF * last)
        q = q_ref[at : at + 64, :]
        new = q - count * q + DT * r_u
        t_out[at : at + 64, :] = new
        lam = a_ref[at : at + 64, :] + new
        a_out[at : at + 64, :] = lam
        l_h, l_l = split(lam)
        x2[at : at + 64, :] = l_h
        x2[320 + at : 384 + at, :] = l_l
        ztop.append(lam[48:64])
        zbot.append(lam[0:16])
    ztop.append(lam_p[48:64])
    zbot.append(lam_p[0:16])

    copies2 = []
    zboth = []
    for way in range(2):
        both = stack(jnp.concatenate(ztop if way == 0 else zbot, 0))
        zboth.append(both)
        gathered = dot(both, exps[way])
        send2[way] = gathered[:80] + gathered[80:]
        copy = remote(send2.at[way], recv2.at[way], ssem2.at[way], rsem2.at[way], 1 - 2 * way)
        copy.start()
        copies2.append(copy)

    term = bulk * wide(mass_ref[...]) * lam_p * sense
    total = term[0:8]
    for i in range(1, 8):
        total = total + term[8 * i : 8 * i + 8]
    block_term = dot_nt(stack(total), repeat)
    block_term = block_term[:8] + block_term[8:]
    parts = jnp.concatenate([jnp.where(where == o, block_term, 0.0) for o in range(span)], 0)
    owned = dot_nt(stack(parts), cell_hot)
    owned = owned[: 8 * span] + owned[8 * span :]
    hsend[...] = owned.reshape(span, 8, cells)
    hcopies = []
    for i, s in enumerate(steps):
        copy = remote(hsend.at[REACH + s], hrecv.at[i], hssem.at[i], hrsem.at[i], s)
        copy.start()
        hcopies.append(copy)

    for way in range(2):
        inside = dot(zboth[way], hots[4 + way])
        wz[way] = inside[:80] + inside[80:]
    t_h = dot(sel_a[...], x2[0:320, :]).astype(BF16)
    t_l = dot(sel_a[...], x2[320:640, :]).astype(BF16)
    x2[256:512, :] = x2[320:576, :]
    for f in range(4):
        rows = slice(80 * f, 80 * f + 80)
        far = dot(jnp.concatenate([t_h[rows], t_l[rows]], 0), hots[f]).astype(BF16)
        x2[512 + 80 * f : 592 + 80 * f, :] = far[0:80]
        x2[832 + 80 * f : 912 + 80 * f, :] = far[80:160]
    result = dot(adj_m[...], x2[...]) + dot(adj_l[...], x2[0:256, :])

    for way in range(2):
        copies2[way].wait()
        outside = dot(stack(recv2[way]), ghots[way])
        wz[way] = wz[way] + outside[:80] + outside[80:]
    low, high = wz[0], wz[1]
    for k in range(4):
        at = 64 * k
        if k == 0:
            first = low[64:80] - low[48:64]
            last = high[64:80] + high[48:64]
        else:
            first, last = low[16 * k : 16 * k + 16], high[16 * k : 16 * k + 16]
            if k == 3:
                first = first - low[0:16]
                last = last + high[0:16]
        r = z_add(result[at : at + 64], HALF * first, HALF * last)
        lam = a_out[at : at + 64, :]
        a_out[at : at + 64, :] = lam - count * lam + DT * r

    for copy in hcopies:
        copy.wait()
    total = hsend[REACH]
    for i in range(len(steps)):
        total = total + hrecv[i]
    h_out[...] = jnp.sum(total, 0, keepdims=True)


def solution(mesh):
    axes = ("elem", "blk")
    devices = mesh.shape["elem"] * mesh.shape["blk"]
    n_blk = mesh.shape["blk"]
    consts = tables()

    def local(tangent, forward, adjoint, bulk, param, neighbours, exports, param_map):
        vmem = pl.BlockSpec(memory_space=pltpu.VMEM)
        span = 2 * REACH + 1
        cells = param.shape[0]
        dma = pltpu.SemaphoreType.DMA
        t_out, a_out, h_out = pl.pallas_call(
            functools.partial(kernel, devices, n_blk),
            out_shape=(
                jax.ShapeDtypeStruct((256, 512), F32),
                jax.ShapeDtypeStruct((256, 512), F32),
                jax.ShapeDtypeStruct((1, cells), F32),
            ),
            in_specs=[vmem] * (8 + len(consts)),
            out_specs=(vmem,) * 3,
            scratch_shapes=[
                pltpu.VMEM((6, 512, 512), BF16),
                pltpu.VMEM((2, 256, 512), BF16),
                pltpu.VMEM((2, 512, 256), BF16),
                pltpu.VMEM((1024, 512), BF16),
                pltpu.VMEM((512, 512), BF16),
                pltpu.VMEM((1152, 512), BF16),
                pltpu.VMEM((2, 80, 512), F32),
                pltpu.VMEM((2, 80, 256), F32),
                pltpu.VMEM((2, 80, 256), F32),
                pltpu.VMEM((2, 80, 256), F32),
                pltpu.VMEM((2, 80, 256), F32),
                pltpu.VMEM((span, 8, cells), F32),
                pltpu.VMEM((8, cells), F32),
                pltpu.VMEM((span, 8, cells), F32),
                pltpu.VMEM((2 * REACH, 8, cells), F32),
                dma((2,)),
                dma((2,)),
                dma((2,)),
                dma((2,)),
                dma((2 * REACH,)),
                dma((span,)),
                dma((2 * REACH,)),
                dma((2 * REACH,)),
            ],
            compiler_params=pltpu.CompilerParams(
                collective_id=0, has_side_effects=True, vmem_limit_bytes=48 * 2**20
            ),
        )(
            tangent.reshape(256, 512),
            forward.reshape(256, 512),
            adjoint.reshape(256, 512),
            bulk.reshape(1, 512),
            param.reshape(1, cells),
            neighbours,
            exports,
            param_map.reshape(1, -1),
            *[jnp.asarray(c) for c in consts],
        )
        return (
            t_out.reshape(4, 64, 512),
            a_out.reshape(4, 64, 512),
            h_out.reshape(cells),
        )

    whole = P(None, None, axes)
    row = P(axes)
    return jax.shard_map(
        local,
        mesh=mesh,
        in_specs=(whole, whole, whole, row, row, P(None, axes), P(None, axes), row),
        out_specs=(whole, whole, row),
        check_vma=False,
    )
```

```python
import functools

import jax
import jax.numpy as jnp
import ml_dtypes
import numpy as np
from jax import lax
from jax.experimental import pallas as pl
from jax.experimental.pallas import tpu as pltpu
from jax.sharding import PartitionSpec as P

BLOCK = 4
REACH = 2
LIFT = 6.0
DT = 0.1
HALF = 0.5 * LIFT
INPUTS = 19
ORDER = (6, 0, 1, 4, 5, 14, 15, 8, 9, 10, 11, 7, 3, 17, 2, 18, 16, 12, 13)
MESH = pl.DeviceIdType.MESH
BF16 = jnp.bfloat16
F32 = jnp.float32


def split_np(matrix):
    high = matrix.astype(np.float32).astype(ml_dtypes.bfloat16)
    low = (matrix - high.astype(np.float64)).astype(np.float32).astype(ml_dtypes.bfloat16)
    return high, low


def tables():
    points = np.array([-1.0, -1.0 / np.sqrt(5.0), 1.0 / np.sqrt(5.0), 1.0])
    one = np.zeros((4, 4))
    for i in range(4):
        for j in range(4):
            if i != j:
                top = np.prod([points[i] - points[k] for k in range(4) if k != i and k != j])
                one[i, j] = top / np.prod([points[j] - points[k] for k in range(4) if k != j])
        one[i, i] = np.sum([1.0 / (points[i] - points[k]) for k in range(4) if k != i])
    eye = np.eye(4)
    deriv = [
        np.kron(np.eye(16), one),
        np.kron(eye, np.kron(one, eye)),
        np.kron(one, np.eye(16)),
    ]
    node = np.arange(64)
    place = [node % 4, node // 4 % 4, node // 16]
    faces = [np.flatnonzero(place[f // 2] == 3 * (f % 2)) for f in range(6)]
    sel = np.zeros((6, 16, 64))
    for f in range(6):
        sel[f, np.arange(16), faces[f]] = 1.0
    count = sel.sum((0, 1))
    local = []
    for d in range(3):
        ends = np.diag(sel[2 * d + 1].sum(0) - sel[2 * d].sum(0))
        local.append(-deriv[d] + HALF * ends)
    weights = np.array([1.0 / 6.0, 5.0 / 6.0, 5.0 / 6.0, 1.0 / 6.0])
    mass = np.kron(weights, np.kron(weights, weights))

    own = np.zeros((256, 256))
    for d in range(3):
        rows = slice(64 + 64 * d, 128 + 64 * d)
        own[:64, rows] = local[d]
        own[rows, :64] = local[d]
    sens = np.concatenate(local, 1)

    sel_t = np.zeros((256, 256))
    sel_f = np.zeros((64, 128))
    sel_a = np.zeros((320, 320))
    lift_t = np.zeros((320, 256))
    lift_s = np.zeros((64, 64))
    lift_a = np.zeros((256, 320))
    for f in range(4):
        d = f // 2
        s = 2.0 * (f % 2) - 1.0
        far = sel[f ^ 1]
        near = sel[f].T
        for k in range(4):
            sel_t[64 * f + 16 * k : 64 * f + 16 * k + 16, 64 * k : 64 * k + 64] = far
        for k in range(5):
            sel_a[80 * f + 16 * k : 80 * f + 16 * k + 16, 64 * k : 64 * k + 64] = far
        sel_f[16 * f : 16 * f + 16, 64 * d : 64 * d + 64] = far
        lift_s[:, 16 * f : 16 * f + 16] = -HALF * s * near
        at = 64 * f
        lift_t[0:64, at : at + 16] += HALF * near
        lift_t[64:128, at + 16 + 16 * d : at + 32 + 16 * d] += -HALF * s * near
        for k in range(3):
            lift_t[128 + 64 * k : 192 + 64 * k, at + 16 + 16 * k : at + 32 + 16 * k] += HALF * near
        lift_t[128 + 64 * d : 192 + 64 * d, at : at + 16] += -HALF * s * near
        at = 80 * f
        lift_a[0:64, at + 64 : at + 80] += HALF * near
        lift_a[0:64, at + 16 + 16 * d : at + 32 + 16 * d] += HALF * s * near
        for k in range(3):
            lift_a[64 + 64 * k : 128 + 64 * k, at + 16 + 16 * k : at + 32 + 16 * k] += HALF * near
        lift_a[64 + 64 * d : 128 + 64 * d, at : at + 16] += HALF * s * near

    own_h, own_l = split_np(own)
    adj_h, adj_l = split_np(own.T)
    sen_h, sen_l = split_np(sens)
    wide = np.zeros((320, 256), own_h.dtype)
    wide[64:] = own_h
    lift_t = lift_t.astype(own_h.dtype)
    lift_s = lift_s.astype(own_h.dtype)
    lift_a = lift_a.astype(own_h.dtype)
    return [
        np.concatenate([wide, wide, lift_t, lift_t], 1),
        own_l,
        np.concatenate([sen_h, sen_h, lift_s, lift_s], 1),
        sen_l,
        np.concatenate([adj_h, adj_h, lift_a, lift_a], 1),
        adj_l,
        sel_t.astype(own_h.dtype),
        sel_f.astype(own_h.dtype),
        sel_a.astype(own_h.dtype),
        np.repeat((DT * HALF * count)[:, None], 128, 1).astype(np.float32),
        np.repeat((2.0 * DT * mass)[:, None], 128, 1).astype(np.float32),
    ]


def dot(a, b):
    return jnp.dot(a, b, preferred_element_type=F32)


def dot_nt(a, b):
    return lax.dot_general(a, b, (((1,), (1,)), ((), ())), preferred_element_type=F32)


def split(value):
    high = value.astype(BF16)
    return high, (value - high.astype(F32)).astype(BF16)


def stack(value):
    return jnp.concatenate(split(value), 0)


def hot(row, rows, base=0):
    width = row.shape[1]
    at = lax.broadcasted_iota(jnp.int32, (rows, width), 0) + base
    return jnp.where(at == row, 1.0, 0.0).astype(BF16)


def wide(column):
    return jnp.concatenate([column] * 4, 1)


def kernel(
    devices,
    n_blk,
    *refs,
):
    sources, refs = refs[:INPUTS], refs[INPUTS:]
    t_out, a_out, h_out = refs[:3]
    refs = refs[3:]
    held, refs = refs[:INPUTS], refs[INPUTS:]
    (
    isem,
    hots,
    ghots,
    exps,
    x1,
    xs,
    x2,
    wz,
    send1,
    recv1,
    send2,
    recv2,
    table,
    psend,
    hsend,
    hrecv,
    ssem1,
    rsem1,
    ssem2,
    rsem2,
    pssem,
    prsem,
    hssem,
    hrsem,
    ) = refs
    (
        q_ref,
        f_ref,
        a_ref,
        k_ref,
        ps_ref,
        nb_ref,
        ex_ref,
        pm_ref,
        main_m,
        main_l,
        sens_m,
        sens_l,
        adj_m,
        adj_l,
        sel_t,
        sel_f,
        sel_a,
        count_ref,
        mass_ref,
    ) = held
    loads = [
        pltpu.make_async_copy(sources[i], held[i], isem.at[i]) for i in range(INPUTS)
    ]
    for i in ORDER:
        loads[i].start()

    def need(*which):
        for i in which:
            loads[i].wait()

    me = lax.axis_index("elem") * n_blk + lax.axis_index("blk")

    def device(step):
        other = lax.rem(me + step + devices, devices)
        return (other // n_blk, lax.rem(other, n_blk))

    steps = [s for s in range(-REACH, REACH + 1) if s]
    barrier = pltpu.get_barrier_semaphore()
    for s in steps:
        pl.semaphore_signal(barrier, inc=1, device_id=device(s), device_id_type=MESH)

    def remote(src, dst, ssem, rsem, step):
        return pltpu.make_async_remote_copy(
            src_ref=src,
            dst_ref=dst,
            send_sem=ssem,
            recv_sem=rsem,
            device_id=device(step),
            device_id_type=MESH,
        )

    def z_trace(refs, top):
        at = 48 if top else 0
        return jnp.concatenate([r[o + at : o + at + 16, :] for r, o in refs], 0)

    fields = [(q_ref, 0), (q_ref, 64), (q_ref, 128), (q_ref, 192), (f_ref, 192)]
    need(6, 0, 1, 4)
    psend[...] = jnp.broadcast_to(ps_ref[...], psend.shape)
    for way in range(2):
        exps[way] = hot(ex_ref[way : way + 1, :], 512)
        both = stack(z_trace(fields, way == 0))
        x2[way * 160 : way * 160 + 160, :] = both
        gathered = dot(both, exps[way])
        send1[way] = gathered[:80] + gathered[80:]
    pl.semaphore_wait(barrier, len(steps))
    copies1 = []
    for way in range(2):
        copy = remote(send1.at[way], recv1.at[way], ssem1.at[way], rsem1.at[way], 1 - 2 * way)
        copy.start()
        copies1.append(copy)
    pcopies = []
    for i, s in enumerate(steps):
        copy = remote(psend, table.at[REACH - s], pssem.at[i], prsem.at[REACH - s], s)
        copy.start()
        pcopies.append(copy)

    need(5)
    for f in range(6):
        hots[f] = hot(nb_ref[f : f + 1, :], 512)
    for way in range(2):
        ghots[way] = hot(nb_ref[4 + way : 5 + way, :], 256, 512)
    q_h, q_l = split(q_ref[...])
    x1[0:256, :] = q_h
    x1[256:512, :] = q_l
    u_h, u_l = split(f_ref[64:256, :])
    xs[0:192, :] = u_h
    xs[192:384, :] = u_l
    for way in range(2):
        inside = dot(x2[way * 160 : way * 160 + 160, :], hots[4 + way])
        wz[way] = inside[:80] + inside[80:]
    need(14, 15)
    t_h = dot(sel_t[...], x1[0:256, :]).astype(BF16)
    t_l = dot(sel_t[...], x1[256:512, :]).astype(BF16)
    tf_h = dot(sel_f[...], xs[0:128, :]).astype(BF16)
    tf_l = dot(sel_f[...], xs[192:320, :]).astype(BF16)
    for f in range(4):
        big = slice(64 * f, 64 * f + 64)
        small = slice(16 * f, 16 * f + 16)
        lhs = jnp.concatenate([t_h[big], t_l[big], tf_h[small], tf_l[small]], 0)
        far = dot(lhs, hots[f]).astype(BF16)
        x1[512 + 64 * f : 576 + 64 * f, :] = far[0:64]
        x1[768 + 64 * f : 832 + 64 * f, :] = far[64:128]
        xs[384 + 16 * f : 400 + 16 * f, :] = far[128:144]
        xs[448 + 16 * f : 464 + 16 * f, :] = far[144:160]
    need(8, 9, 10, 11, 3, 7)
    main = dot(main_m[...], x1[...])
    main_low = dot(main_l[...], x1[0:256, :])
    sense = dot(sens_m[...], xs[...]) + dot(sens_l[...], xs[0:192, :])
    bulk = jnp.broadcast_to(k_ref[...], (64, 512))

    pm = pm_ref[...]
    cells = ps_ref.shape[1]
    owner = pm // cells
    cell = pm - owner * cells
    where = owner - me + REACH
    where = jnp.where(where < 0, where + devices, where)
    where = jnp.where(where >= devices, where - devices, where)
    cell_hot = hot(cell, cells)
    blocks = pm.shape[1]
    repeat = jnp.where(
        lax.broadcasted_iota(jnp.int32, (blocks, 512), 1) // BLOCK
        == lax.broadcasted_iota(jnp.int32, (blocks, 512), 0),
        1.0,
        0.0,
    ).astype(BF16)
    for copy in pcopies:
        copy.wait()
    table[REACH] = psend[...]
    span = 2 * REACH + 1
    picked = dot(stack(table[...].reshape(8 * span, cells)), cell_hot)
    picked = picked[: 8 * span] + picked[8 * span :]
    block_step = jnp.zeros((8, blocks), F32)
    for o in range(span):
        block_step = jnp.where(where == o, picked[8 * o : 8 * o + 8], block_step)
    spread = dot(stack(block_step), repeat)
    step = jnp.concatenate([spread[:8] + spread[8:]] * 8, 0)

    for way in range(2):
        copies1[way].wait()
        outside = dot(stack(recv1[way]), ghots[way])
        wz[way] = wz[way] + outside[:80] + outside[80:]

    low, high = wz[0], wz[1]

    def z_add(value, first, last):
        return jnp.concatenate([value[0:16] + first, value[16:48], value[48:64] + last], 0)

    sense = z_add(sense, HALF * low[64:80], -HALF * high[64:80])
    r_a = z_add(main[0:64], HALF * low[0:16], HALF * high[0:16])
    r_b = z_add(main[64:128] + main_low[0:64], HALF * low[48:64], -HALF * high[48:64])
    r_b = r_b + 2.0 * step * sense
    need(17, 2)
    count = wide(count_ref[...])
    q = q_ref[0:64, :]
    new = q - count * q + DT * (r_a + bulk * r_b)
    t_out[0:64, :] = new
    lam = a_ref[0:64, :] + new
    lam_p = lam
    k_lam = bulk * lam
    a_out[0:64, :] = lam
    k_h, k_l = split(k_lam)
    p_h, p_l = split(lam)
    x2[0:64, :] = k_h
    x2[320:384, :] = k_l
    x2[256:320, :] = p_h
    x2[576:640, :] = p_l
    ztop = [k_lam[48:64]]
    zbot = [k_lam[0:16]]
    for k in range(3):
        at = 64 + 64 * k
        first, last = low[16 + 16 * k : 32 + 16 * k], high[16 + 16 * k : 32 + 16 * k]
        if k == 2:
            first = first + low[0:16]
            last = last - high[0:16]
        r_u = z_add(main[64 + at : 128 + at] + main_low[at : at + 64], HALF * first, HALF * last)
        q = q_ref[at : at + 64, :]
        new = q - count * q + DT * r_u
        t_out[at : at + 64, :] = new
        lam = a_ref[at : at + 64, :] + new
        a_out[at : at + 64, :] = lam
        l_h, l_l = split(lam)
        x2[at : at + 64, :] = l_h
        x2[320 + at : 384 + at, :] = l_l
        ztop.append(lam[48:64])
        zbot.append(lam[0:16])
    ztop.append(lam_p[48:64])
    zbot.append(lam_p[0:16])

    copies2 = []
    zboth = []
    for way in range(2):
        both = stack(jnp.concatenate(ztop if way == 0 else zbot, 0))
        zboth.append(both)
        gathered = dot(both, exps[way])
        send2[way] = gathered[:80] + gathered[80:]
        copy = remote(send2.at[way], recv2.at[way], ssem2.at[way], rsem2.at[way], 1 - 2 * way)
        copy.start()
        copies2.append(copy)

    need(18)
    term = bulk * wide(mass_ref[...]) * lam_p * sense
    total = term[0:8]
    for i in range(1, 8):
        total = total + term[8 * i : 8 * i + 8]
    block_term = dot_nt(stack(total), repeat)
    block_term = block_term[:8] + block_term[8:]
    parts = jnp.concatenate([jnp.where(where == o, block_term, 0.0) for o in range(span)], 0)
    owned = dot_nt(stack(parts), cell_hot)
    owned = owned[: 8 * span] + owned[8 * span :]
    hsend[...] = owned.reshape(span, 8, cells)
    hcopies = []
    for i, s in enumerate(steps):
        copy = remote(hsend.at[REACH + s], hrecv.at[i], hssem.at[i], hrsem.at[i], s)
        copy.start()
        hcopies.append(copy)

    need(16, 12, 13)
    for way in range(2):
        inside = dot(zboth[way], hots[4 + way])
        wz[way] = inside[:80] + inside[80:]
    t_h = dot(sel_a[...], x2[0:320, :]).astype(BF16)
    t_l = dot(sel_a[...], x2[320:640, :]).astype(BF16)
    x2[256:512, :] = x2[320:576, :]
    for f in range(4):
        rows = slice(80 * f, 80 * f + 80)
        far = dot(jnp.concatenate([t_h[rows], t_l[rows]], 0), hots[f]).astype(BF16)
        x2[512 + 80 * f : 592 + 80 * f, :] = far[0:80]
        x2[832 + 80 * f : 912 + 80 * f, :] = far[80:160]
    result = dot(adj_m[...], x2[...]) + dot(adj_l[...], x2[0:256, :])

    for way in range(2):
        copies2[way].wait()
        outside = dot(stack(recv2[way]), ghots[way])
        wz[way] = wz[way] + outside[:80] + outside[80:]
    low, high = wz[0], wz[1]
    for k in range(4):
        at = 64 * k
        if k == 0:
            first = low[64:80] - low[48:64]
            last = high[64:80] + high[48:64]
        else:
            first, last = low[16 * k : 16 * k + 16], high[16 * k : 16 * k + 16]
            if k == 3:
                first = first - low[0:16]
                last = last + high[0:16]
        r = z_add(result[at : at + 64], HALF * first, HALF * last)
        lam = a_out[at : at + 64, :]
        a_out[at : at + 64, :] = lam - count * lam + DT * r

    for copy in hcopies:
        copy.wait()
    total = hsend[REACH]
    for i in range(len(steps)):
        total = total + hrecv[i]
    h_out[...] = jnp.sum(total, 0, keepdims=True)


def solution(mesh):
    axes = ("elem", "blk")
    devices = mesh.shape["elem"] * mesh.shape["blk"]
    n_blk = mesh.shape["blk"]
    consts = tables()

    def local(tangent, forward, adjoint, bulk, param, neighbours, exports, param_map):
        hbm = pl.BlockSpec(memory_space=pltpu.HBM)
        vmem = pl.BlockSpec(memory_space=pltpu.VMEM)
        args = [
            tangent.reshape(256, 512),
            forward.reshape(256, 512),
            adjoint.reshape(256, 512),
            bulk.reshape(1, 512),
            param.reshape(1, -1),
            neighbours,
            exports,
            param_map.reshape(1, -1),
            *[jnp.asarray(c) for c in consts],
        ]
        span = 2 * REACH + 1
        cells = param.shape[0]
        dma = pltpu.SemaphoreType.DMA
        t_out, a_out, h_out = pl.pallas_call(
            functools.partial(kernel, devices, n_blk),
            out_shape=(
                jax.ShapeDtypeStruct((256, 512), F32),
                jax.ShapeDtypeStruct((256, 512), F32),
                jax.ShapeDtypeStruct((1, cells), F32),
            ),
            in_specs=[hbm] * INPUTS,
            out_specs=(vmem,) * 3,
            scratch_shapes=[pltpu.VMEM(a.shape, a.dtype) for a in args]
            + [
                dma((INPUTS,)),
                pltpu.VMEM((6, 512, 512), BF16),
                pltpu.VMEM((2, 256, 512), BF16),
                pltpu.VMEM((2, 512, 256), BF16),
                pltpu.VMEM((1024, 512), BF16),
                pltpu.VMEM((512, 512), BF16),
                pltpu.VMEM((1152, 512), BF16),
                pltpu.VMEM((2, 80, 512), F32),
                pltpu.VMEM((2, 80, 256), F32),
                pltpu.VMEM((2, 80, 256), F32),
                pltpu.VMEM((2, 80, 256), F32),
                pltpu.VMEM((2, 80, 256), F32),
                pltpu.VMEM((span, 8, cells), F32),
                pltpu.VMEM((8, cells), F32),
                pltpu.VMEM((span, 8, cells), F32),
                pltpu.VMEM((2 * REACH, 8, cells), F32),
                dma((2,)),
                dma((2,)),
                dma((2,)),
                dma((2,)),
                dma((2 * REACH,)),
                dma((span,)),
                dma((2 * REACH,)),
                dma((2 * REACH,)),
            ],
            compiler_params=pltpu.CompilerParams(
                collective_id=0, has_side_effects=True, vmem_limit_bytes=40 * 2**20
            ),
        )(*args)
        return (
            t_out.reshape(4, 64, 512),
            a_out.reshape(4, 64, 512),
            h_out.reshape(cells),
        )

    whole = P(None, None, axes)
    row = P(axes)
    return jax.shard_map(
        local,
        mesh=mesh,
        in_specs=(whole, whole, whole, row, row, P(None, axes), P(None, axes), row),
        out_specs=(whole, whole, row),
        check_vma=False,
    )
```

```python
import functools

import jax
import jax.numpy as jnp
import ml_dtypes
import numpy as np
from jax import lax
from jax.experimental import pallas as pl
from jax.experimental.pallas import tpu as pltpu
from jax.sharding import PartitionSpec as P

BLOCK = 4
REACH = 2
LIFT = 6.0
DT = 0.1
HALF = 0.5 * LIFT
INPUTS = 19
ORDER = (6, 0, 1, 4, 5, 14, 15, 8, 9, 10, 11, 7, 3, 17, 2, 18, 16, 12, 13)
MESH = pl.DeviceIdType.MESH
BF16 = jnp.bfloat16
F32 = jnp.float32


def split_np(matrix):
    high = matrix.astype(np.float32).astype(ml_dtypes.bfloat16)
    low = (matrix - high.astype(np.float64)).astype(np.float32).astype(ml_dtypes.bfloat16)
    return high, low


def tables():
    points = np.array([-1.0, -1.0 / np.sqrt(5.0), 1.0 / np.sqrt(5.0), 1.0])
    one = np.zeros((4, 4))
    for i in range(4):
        for j in range(4):
            if i != j:
                top = np.prod([points[i] - points[k] for k in range(4) if k != i and k != j])
                one[i, j] = top / np.prod([points[j] - points[k] for k in range(4) if k != j])
        one[i, i] = np.sum([1.0 / (points[i] - points[k]) for k in range(4) if k != i])
    eye = np.eye(4)
    deriv = [
        np.kron(np.eye(16), one),
        np.kron(eye, np.kron(one, eye)),
        np.kron(one, np.eye(16)),
    ]
    node = np.arange(64)
    place = [node % 4, node // 4 % 4, node // 16]
    faces = [np.flatnonzero(place[f // 2] == 3 * (f % 2)) for f in range(6)]
    sel = np.zeros((6, 16, 64))
    for f in range(6):
        sel[f, np.arange(16), faces[f]] = 1.0
    count = sel.sum((0, 1))
    local = []
    for d in range(3):
        ends = np.diag(sel[2 * d + 1].sum(0) - sel[2 * d].sum(0))
        local.append(-deriv[d] + HALF * ends)
    weights = np.array([1.0 / 6.0, 5.0 / 6.0, 5.0 / 6.0, 1.0 / 6.0])
    mass = np.kron(weights, np.kron(weights, weights))

    own = np.zeros((256, 256))
    for d in range(3):
        rows = slice(64 + 64 * d, 128 + 64 * d)
        own[:64, rows] = local[d]
        own[rows, :64] = local[d]
    sens = np.concatenate(local, 1)

    sel_t = np.zeros((256, 256))
    sel_f = np.zeros((64, 128))
    sel_a = np.zeros((320, 320))
    lift_t = np.zeros((320, 256))
    lift_s = np.zeros((64, 64))
    lift_a = np.zeros((256, 320))
    for f in range(4):
        d = f // 2
        s = 2.0 * (f % 2) - 1.0
        far = sel[f ^ 1]
        near = sel[f].T
        for k in range(4):
            sel_t[64 * f + 16 * k : 64 * f + 16 * k + 16, 64 * k : 64 * k + 64] = far
        for k in range(5):
            sel_a[80 * f + 16 * k : 80 * f + 16 * k + 16, 64 * k : 64 * k + 64] = far
        sel_f[16 * f : 16 * f + 16, 64 * d : 64 * d + 64] = far
        lift_s[:, 16 * f : 16 * f + 16] = -HALF * s * near
        at = 64 * f
        lift_t[0:64, at : at + 16] += HALF * near
        lift_t[64:128, at + 16 + 16 * d : at + 32 + 16 * d] += -HALF * s * near
        for k in range(3):
            lift_t[128 + 64 * k : 192 + 64 * k, at + 16 + 16 * k : at + 32 + 16 * k] += HALF * near
        lift_t[128 + 64 * d : 192 + 64 * d, at : at + 16] += -HALF * s * near
        at = 80 * f
        lift_a[0:64, at + 64 : at + 80] += HALF * near
        lift_a[0:64, at + 16 + 16 * d : at + 32 + 16 * d] += HALF * s * near
        for k in range(3):
            lift_a[64 + 64 * k : 128 + 64 * k, at + 16 + 16 * k : at + 32 + 16 * k] += HALF * near
        lift_a[64 + 64 * d : 128 + 64 * d, at : at + 16] += HALF * s * near

    own_h, own_l = split_np(own)
    adj_h, adj_l = split_np(own.T)
    sen_h, sen_l = split_np(sens)
    wide = np.zeros((320, 256), own_h.dtype)
    wide[64:] = own_h
    lift_t = lift_t.astype(own_h.dtype)
    lift_s = lift_s.astype(own_h.dtype)
    lift_a = lift_a.astype(own_h.dtype)
    return [
        np.concatenate([wide, wide, lift_t, lift_t], 1),
        own_l,
        np.concatenate([sen_h, sen_h, lift_s, lift_s], 1),
        sen_l,
        np.concatenate([adj_h, adj_h, lift_a, lift_a], 1),
        adj_l,
        sel_t.astype(own_h.dtype),
        sel_f.astype(own_h.dtype),
        sel_a.astype(own_h.dtype),
        np.repeat((DT * HALF * count)[:, None], 128, 1).astype(np.float32),
        np.repeat((2.0 * DT * mass)[:, None], 128, 1).astype(np.float32),
    ]


def dot(a, b):
    return jnp.dot(a, b, preferred_element_type=F32)


def dot_nt(a, b):
    return lax.dot_general(a, b, (((1,), (1,)), ((), ())), preferred_element_type=F32)


def split(value):
    high = value.astype(BF16)
    return high, (value - high.astype(F32)).astype(BF16)


def stack(value):
    return jnp.concatenate(split(value), 0)


def hot(row, rows, base=0):
    width = row.shape[1]
    at = lax.broadcasted_iota(jnp.int32, (rows, width), 0) + base
    return jnp.where(at == row, 1.0, 0.0).astype(BF16)


def wide(column):
    return jnp.concatenate([column] * 4, 1)


def kernel(
    devices,
    n_blk,
    *refs,
):
    sources, refs = refs[:INPUTS], refs[INPUTS:]
    t_out, a_out, h_out = refs[:3]
    refs = refs[3:]
    held, refs = refs[:INPUTS], refs[INPUTS:]
    (
    isem,
    hots,
    ghots,
    exps,
    x1,
    xs,
    x2,
    wz,
    send1,
    recv1,
    send2,
    recv2,
    table,
    psend,
    hsend,
    hrecv,
    ssem1,
    rsem1,
    ssem2,
    rsem2,
    pssem,
    prsem,
    hssem,
    hrsem,
    ) = refs
    (
        q_ref,
        f_ref,
        a_ref,
        k_ref,
        ps_ref,
        nb_ref,
        ex_ref,
        pm_ref,
        main_m,
        main_l,
        sens_m,
        sens_l,
        adj_m,
        adj_l,
        sel_t,
        sel_f,
        sel_a,
        count_ref,
        mass_ref,
    ) = held
    loads = [
        pltpu.make_async_copy(sources[i], held[i], isem.at[i]) for i in range(INPUTS)
    ]
    for i in ORDER:
        loads[i].start()

    def need(*which):
        for i in which:
            loads[i].wait()

    me = lax.axis_index("elem") * n_blk + lax.axis_index("blk")

    def device(step):
        other = lax.rem(me + step + devices, devices)
        return (other // n_blk, lax.rem(other, n_blk))

    steps = [s for s in range(-REACH, REACH + 1) if s]
    barrier = pltpu.get_barrier_semaphore()
    for s in steps:
        pl.semaphore_signal(barrier, inc=1, device_id=device(s), device_id_type=MESH)

    def remote(src, dst, ssem, rsem, step):
        return pltpu.make_async_remote_copy(
            src_ref=src,
            dst_ref=dst,
            send_sem=ssem,
            recv_sem=rsem,
            device_id=device(step),
            device_id_type=MESH,
        )

    def z_trace(refs, top):
        at = 48 if top else 0
        return jnp.concatenate([r[o + at : o + at + 16, :] for r, o in refs], 0)

    fields = [(q_ref, 0), (q_ref, 64), (q_ref, 128), (q_ref, 192), (f_ref, 192)]
    need(6, 0, 1, 4)
    psend[...] = jnp.broadcast_to(ps_ref[...], psend.shape)
    for way in range(2):
        exps[way] = hot(ex_ref[way : way + 1, :], 512)
        both = stack(z_trace(fields, way == 0))
        x2[way * 160 : way * 160 + 160, :] = both
        gathered = dot(both, exps[way])
        send1[way] = gathered[:80] + gathered[80:]
    pl.semaphore_wait(barrier, len(steps))
    copies1 = []
    for way in range(2):
        copy = remote(send1.at[way], recv1.at[way], ssem1.at[way], rsem1.at[way], 1 - 2 * way)
        copy.start()
        copies1.append(copy)
    pcopies = []
    for i, s in enumerate(steps):
        copy = remote(psend, table.at[REACH - s], pssem.at[i], prsem.at[REACH - s], s)
        copy.start()
        pcopies.append(copy)

    need(5)
    for f in range(6):
        hots[f] = hot(nb_ref[f : f + 1, :], 512)
    for way in range(2):
        ghots[way] = hot(nb_ref[4 + way : 5 + way, :], 256, 512)
    q_h, q_l = split(q_ref[...])
    x1[0:256, :] = q_h
    x1[256:512, :] = q_l
    u_h, u_l = split(f_ref[64:256, :])
    xs[0:192, :] = u_h
    xs[192:384, :] = u_l
    for way in range(2):
        inside = dot(x2[way * 160 : way * 160 + 160, :], hots[4 + way])
        wz[way] = inside[:80] + inside[80:]
    need(14, 15)
    t_h = dot(sel_t[...], x1[0:256, :]).astype(BF16)
    t_l = dot(sel_t[...], x1[256:512, :]).astype(BF16)
    tf_h = dot(sel_f[...], xs[0:128, :]).astype(BF16)
    tf_l = dot(sel_f[...], xs[192:320, :]).astype(BF16)
    for f in range(4):
        big = slice(64 * f, 64 * f + 64)
        small = slice(16 * f, 16 * f + 16)
        lhs = jnp.concatenate([t_h[big], t_l[big], tf_h[small], tf_l[small]], 0)
        far = dot(lhs, hots[f]).astype(BF16)
        x1[512 + 64 * f : 576 + 64 * f, :] = far[0:64]
        x1[768 + 64 * f : 832 + 64 * f, :] = far[64:128]
        xs[384 + 16 * f : 400 + 16 * f, :] = far[128:144]
        xs[448 + 16 * f : 464 + 16 * f, :] = far[144:160]
    need(8, 9, 10, 11, 3, 7)
    main = dot(main_m[...], x1[...])
    main_low = dot(main_l[...], x1[0:256, :])
    sense = dot(sens_m[...], xs[...]) + dot(sens_l[...], xs[0:192, :])
    bulk = jnp.broadcast_to(k_ref[...], (64, 512))

    pm = pm_ref[...]
    cells = ps_ref.shape[1]
    owner = pm // cells
    cell = pm - owner * cells
    where = owner - me + REACH
    where = jnp.where(where < 0, where + devices, where)
    where = jnp.where(where >= devices, where - devices, where)
    cell_hot = hot(cell, cells)
    blocks = pm.shape[1]
    repeat = jnp.where(
        lax.broadcasted_iota(jnp.int32, (blocks, 512), 1) // BLOCK
        == lax.broadcasted_iota(jnp.int32, (blocks, 512), 0),
        1.0,
        0.0,
    ).astype(BF16)
    for copy in pcopies:
        copy.wait()
    table[REACH] = psend[...]
    span = 2 * REACH + 1
    picked = dot(stack(table[...].reshape(8 * span, cells)), cell_hot)
    picked = picked[: 8 * span] + picked[8 * span :]
    block_step = jnp.zeros((8, blocks), F32)
    for o in range(span):
        block_step = jnp.where(where == o, picked[8 * o : 8 * o + 8], block_step)
    spread = dot(stack(block_step), repeat)
    step = jnp.concatenate([spread[:8] + spread[8:]] * 8, 0)

    for way in range(2):
        copies1[way].wait()
        outside = dot(stack(recv1[way]), ghots[way])
        wz[way] = wz[way] + outside[:80] + outside[80:]

    low, high = wz[0], wz[1]

    def z_add(value, first, last):
        return jnp.concatenate([value[0:16] + first, value[16:48], value[48:64] + last], 0)

    sense = z_add(sense, HALF * low[64:80], -HALF * high[64:80])
    r_a = z_add(main[0:64], HALF * low[0:16], HALF * high[0:16])
    r_b = z_add(main[64:128] + main_low[0:64], HALF * low[48:64], -HALF * high[48:64])
    r_b = r_b + 2.0 * step * sense
    need(17, 2)
    count = wide(count_ref[...])
    q = q_ref[0:64, :]
    new = q - count * q + DT * (r_a + bulk * r_b)
    t_out[0:64, :] = new
    lam = a_ref[0:64, :] + new
    lam_p = lam
    k_lam = bulk * lam
    a_out[0:64, :] = lam
    k_h, k_l = split(k_lam)
    p_h, p_l = split(lam)
    x2[0:64, :] = k_h
    x2[320:384, :] = k_l
    x2[256:320, :] = p_h
    x2[576:640, :] = p_l
    ztop = [k_lam[48:64]]
    zbot = [k_lam[0:16]]
    for k in range(3):
        at = 64 + 64 * k
        first, last = low[16 + 16 * k : 32 + 16 * k], high[16 + 16 * k : 32 + 16 * k]
        if k == 2:
            first = first + low[0:16]
            last = last - high[0:16]
        r_u = z_add(main[64 + at : 128 + at] + main_low[at : at + 64], HALF * first, HALF * last)
        q = q_ref[at : at + 64, :]
        new = q - count * q + DT * r_u
        t_out[at : at + 64, :] = new
        lam = a_ref[at : at + 64, :] + new
        a_out[at : at + 64, :] = lam
        l_h, l_l = split(lam)
        x2[at : at + 64, :] = l_h
        x2[320 + at : 384 + at, :] = l_l
        ztop.append(lam[48:64])
        zbot.append(lam[0:16])
    ztop.append(lam_p[48:64])
    zbot.append(lam_p[0:16])

    copies2 = []
    zboth = []
    for way in range(2):
        both = stack(jnp.concatenate(ztop if way == 0 else zbot, 0))
        zboth.append(both)
        gathered = dot(both, exps[way])
        send2[way] = gathered[:80] + gathered[80:]
        copy = remote(send2.at[way], recv2.at[way], ssem2.at[way], rsem2.at[way], 1 - 2 * way)
        copy.start()
        copies2.append(copy)

    need(18)
    term = bulk * wide(mass_ref[...]) * lam_p * sense
    total = term[0:8]
    for i in range(1, 8):
        total = total + term[8 * i : 8 * i + 8]
    block_term = dot_nt(stack(total), repeat)
    block_term = block_term[:8] + block_term[8:]
    parts = jnp.concatenate([jnp.where(where == o, block_term, 0.0) for o in range(span)], 0)
    owned = dot_nt(stack(parts), cell_hot)
    owned = owned[: 8 * span] + owned[8 * span :]
    hsend[...] = owned.reshape(span, 8, cells)
    hcopies = []
    for i, s in enumerate(steps):
        copy = remote(hsend.at[REACH + s], hrecv.at[i], hssem.at[i], hrsem.at[i], s)
        copy.start()
        hcopies.append(copy)

    need(16, 12, 13)
    for way in range(2):
        inside = dot(zboth[way], hots[4 + way])
        wz[way] = inside[:80] + inside[80:]
    t_h = dot(sel_a[...], x2[0:320, :]).astype(BF16)
    t_l = dot(sel_a[...], x2[320:640, :]).astype(BF16)
    x2[256:512, :] = x2[320:576, :]
    for f in range(4):
        rows = slice(80 * f, 80 * f + 80)
        far = dot(jnp.concatenate([t_h[rows], t_l[rows]], 0), hots[f]).astype(BF16)
        x2[512 + 80 * f : 592 + 80 * f, :] = far[0:80]
        x2[832 + 80 * f : 912 + 80 * f, :] = far[80:160]
    result = dot(adj_m[...], x2[...]) + dot(adj_l[...], x2[0:256, :])

    for way in range(2):
        copies2[way].wait()
        outside = dot(stack(recv2[way]), ghots[way])
        wz[way] = wz[way] + outside[:80] + outside[80:]
    low, high = wz[0], wz[1]
    for k in range(4):
        at = 64 * k
        if k == 0:
            first = low[64:80] - low[48:64]
            last = high[64:80] + high[48:64]
        else:
            first, last = low[16 * k : 16 * k + 16], high[16 * k : 16 * k + 16]
            if k == 3:
                first = first - low[0:16]
                last = last + high[0:16]
        r = z_add(result[at : at + 64], HALF * first, HALF * last)
        lam = a_out[at : at + 64, :]
        a_out[at : at + 64, :] = lam - count * lam + DT * r

    for copy in hcopies:
        copy.wait()
    total = hsend[REACH]
    for i in range(len(steps)):
        total = total + hrecv[i]
    h_out[...] = jnp.sum(total, 0, keepdims=True)


def solution(mesh):
    axes = ("elem", "blk")
    devices = mesh.shape["elem"] * mesh.shape["blk"]
    n_blk = mesh.shape["blk"]
    consts = tables()

    def local(tangent, forward, adjoint, bulk, param, neighbours, exports, param_map):
        hbm = pl.BlockSpec(memory_space=pltpu.HBM)
        vmem = pl.BlockSpec(memory_space=pltpu.VMEM)
        args = [
            tangent.reshape(256, 512),
            forward.reshape(256, 512),
            adjoint.reshape(256, 512),
            bulk.reshape(1, 512),
            param.reshape(1, -1),
            neighbours,
            exports,
            param_map.reshape(1, -1),
            *[jnp.asarray(c) for c in consts],
        ]
        span = 2 * REACH + 1
        cells = param.shape[0]
        dma = pltpu.SemaphoreType.DMA
        t_out, a_out, h_out = pl.pallas_call(
            functools.partial(kernel, devices, n_blk),
            out_shape=(
                jax.ShapeDtypeStruct((256, 512), F32),
                jax.ShapeDtypeStruct((256, 512), F32),
                jax.ShapeDtypeStruct((1, cells), F32),
            ),
            in_specs=[hbm] * INPUTS,
            out_specs=(vmem,) * 3,
            scratch_shapes=[pltpu.VMEM(a.shape, a.dtype) for a in args]
            + [
                dma((INPUTS,)),
                pltpu.VMEM((6, 512, 512), BF16),
                pltpu.VMEM((2, 256, 512), BF16),
                pltpu.VMEM((2, 512, 256), BF16),
                pltpu.VMEM((1024, 512), BF16),
                pltpu.VMEM((512, 512), BF16),
                pltpu.VMEM((1152, 512), BF16),
                pltpu.VMEM((2, 80, 512), F32),
                pltpu.VMEM((2, 80, 256), F32),
                pltpu.VMEM((2, 80, 256), F32),
                pltpu.VMEM((2, 80, 256), F32),
                pltpu.VMEM((2, 80, 256), F32),
                pltpu.VMEM((span, 8, cells), F32),
                pltpu.VMEM((8, cells), F32),
                pltpu.VMEM((span, 8, cells), F32),
                pltpu.VMEM((2 * REACH, 8, cells), F32),
                dma((2,)),
                dma((2,)),
                dma((2,)),
                dma((2,)),
                dma((2 * REACH,)),
                dma((span,)),
                dma((2 * REACH,)),
                dma((2 * REACH,)),
            ],
            compiler_params=pltpu.CompilerParams(
                collective_id=0, has_side_effects=True, vmem_limit_bytes=62 * 2**20
            ),
        )(*args)
        return (
            t_out.reshape(4, 64, 512),
            a_out.reshape(4, 64, 512),
            h_out.reshape(cells),
        )

    whole = P(None, None, axes)
    row = P(axes)
    return jax.shard_map(
        local,
        mesh=mesh,
        in_specs=(whole, whole, whole, row, row, P(None, axes), P(None, axes), row),
        out_specs=(whole, whole, row),
        check_vma=False,
    )
```

```python
import functools

import jax
import jax.numpy as jnp
import ml_dtypes
import numpy as np
from jax import lax
from jax.experimental import pallas as pl
from jax.experimental.pallas import tpu as pltpu
from jax.sharding import PartitionSpec as P

BLOCK = 4
REACH = 2
LIFT = 6.0
DT = 0.1
HALF = 0.5 * LIFT
INPUTS = 19
EARLY = (6, 0, 1, 4, 5)
LATE = (14, 15, 8, 9, 10, 11, 7, 3, 17, 2, 18, 16, 12, 13)
MESH = pl.DeviceIdType.MESH
BF16 = jnp.bfloat16
F32 = jnp.float32


def split_np(matrix):
    high = matrix.astype(np.float32).astype(ml_dtypes.bfloat16)
    low = (matrix - high.astype(np.float64)).astype(np.float32).astype(ml_dtypes.bfloat16)
    return high, low


def tables():
    points = np.array([-1.0, -1.0 / np.sqrt(5.0), 1.0 / np.sqrt(5.0), 1.0])
    one = np.zeros((4, 4))
    for i in range(4):
        for j in range(4):
            if i != j:
                top = np.prod([points[i] - points[k] for k in range(4) if k != i and k != j])
                one[i, j] = top / np.prod([points[j] - points[k] for k in range(4) if k != j])
        one[i, i] = np.sum([1.0 / (points[i] - points[k]) for k in range(4) if k != i])
    eye = np.eye(4)
    deriv = [
        np.kron(np.eye(16), one),
        np.kron(eye, np.kron(one, eye)),
        np.kron(one, np.eye(16)),
    ]
    node = np.arange(64)
    place = [node % 4, node // 4 % 4, node // 16]
    faces = [np.flatnonzero(place[f // 2] == 3 * (f % 2)) for f in range(6)]
    sel = np.zeros((6, 16, 64))
    for f in range(6):
        sel[f, np.arange(16), faces[f]] = 1.0
    count = sel.sum((0, 1))
    local = []
    for d in range(3):
        ends = np.diag(sel[2 * d + 1].sum(0) - sel[2 * d].sum(0))
        local.append(-deriv[d] + HALF * ends)
    weights = np.array([1.0 / 6.0, 5.0 / 6.0, 5.0 / 6.0, 1.0 / 6.0])
    mass = np.kron(weights, np.kron(weights, weights))

    own = np.zeros((256, 256))
    for d in range(3):
        rows = slice(64 + 64 * d, 128 + 64 * d)
        own[:64, rows] = local[d]
        own[rows, :64] = local[d]
    sens = np.concatenate(local, 1)

    sel_t = np.zeros((256, 256))
    sel_f = np.zeros((64, 128))
    sel_a = np.zeros((320, 320))
    lift_t = np.zeros((320, 256))
    lift_s = np.zeros((64, 64))
    lift_a = np.zeros((256, 320))
    for f in range(4):
        d = f // 2
        s = 2.0 * (f % 2) - 1.0
        far = sel[f ^ 1]
        near = sel[f].T
        for k in range(4):
            sel_t[64 * f + 16 * k : 64 * f + 16 * k + 16, 64 * k : 64 * k + 64] = far
        for k in range(5):
            sel_a[80 * f + 16 * k : 80 * f + 16 * k + 16, 64 * k : 64 * k + 64] = far
        sel_f[16 * f : 16 * f + 16, 64 * d : 64 * d + 64] = far
        lift_s[:, 16 * f : 16 * f + 16] = -HALF * s * near
        at = 64 * f
        lift_t[0:64, at : at + 16] += HALF * near
        lift_t[64:128, at + 16 + 16 * d : at + 32 + 16 * d] += -HALF * s * near
        for k in range(3):
            lift_t[128 + 64 * k : 192 + 64 * k, at + 16 + 16 * k : at + 32 + 16 * k] += HALF * near
        lift_t[128 + 64 * d : 192 + 64 * d, at : at + 16] += -HALF * s * near
        at = 80 * f
        lift_a[0:64, at + 64 : at + 80] += HALF * near
        lift_a[0:64, at + 16 + 16 * d : at + 32 + 16 * d] += HALF * s * near
        for k in range(3):
            lift_a[64 + 64 * k : 128 + 64 * k, at + 16 + 16 * k : at + 32 + 16 * k] += HALF * near
        lift_a[64 + 64 * d : 128 + 64 * d, at : at + 16] += HALF * s * near

    own_h, own_l = split_np(own)
    adj_h, adj_l = split_np(own.T)
    sen_h, sen_l = split_np(sens)
    wide = np.zeros((320, 256), own_h.dtype)
    wide[64:] = own_h
    lift_t = lift_t.astype(own_h.dtype)
    lift_s = lift_s.astype(own_h.dtype)
    lift_a = lift_a.astype(own_h.dtype)
    return [
        np.concatenate([wide, wide, lift_t, lift_t], 1),
        own_l,
        np.concatenate([sen_h, sen_h, lift_s, lift_s], 1),
        sen_l,
        np.concatenate([adj_h, adj_h, lift_a, lift_a], 1),
        adj_l,
        sel_t.astype(own_h.dtype),
        sel_f.astype(own_h.dtype),
        sel_a.astype(own_h.dtype),
        np.repeat((DT * HALF * count)[:, None], 128, 1).astype(np.float32),
        np.repeat((2.0 * DT * mass)[:, None], 128, 1).astype(np.float32),
    ]


def dot(a, b):
    return jnp.dot(a, b, preferred_element_type=F32)


def dot_nt(a, b):
    return lax.dot_general(a, b, (((1,), (1,)), ((), ())), preferred_element_type=F32)


def split(value):
    high = value.astype(BF16)
    return high, (value - high.astype(F32)).astype(BF16)


def stack(value):
    return jnp.concatenate(split(value), 0)


def hot(row, rows, base=0):
    width = row.shape[1]
    at = lax.broadcasted_iota(jnp.int32, (rows, width), 0) + base
    return jnp.where(at == row, 1.0, 0.0).astype(BF16)


def wide(column):
    return jnp.concatenate([column] * 4, 1)


def kernel(
    devices,
    n_blk,
    *refs,
):
    sources, refs = refs[:INPUTS], refs[INPUTS:]
    t_out, a_out, h_out = refs[:3]
    refs = refs[3:]
    held, refs = refs[:INPUTS], refs[INPUTS:]
    (
    isem,
    hots,
    ghots,
    exps,
    x1,
    xs,
    x2,
    wz,
    send1,
    recv1,
    send2,
    recv2,
    table,
    psend,
    hsend,
    hrecv,
    ssem1,
    rsem1,
    ssem2,
    rsem2,
    pssem,
    prsem,
    hssem,
    hrsem,
    ) = refs
    (
        q_ref,
        f_ref,
        a_ref,
        k_ref,
        ps_ref,
        nb_ref,
        ex_ref,
        pm_ref,
        main_m,
        main_l,
        sens_m,
        sens_l,
        adj_m,
        adj_l,
        sel_t,
        sel_f,
        sel_a,
        count_ref,
        mass_ref,
    ) = held
    loads = [
        pltpu.make_async_copy(sources[i], held[i], isem.at[i]) for i in range(INPUTS)
    ]
    for i in EARLY:
        loads[i].start()

    def need(*which):
        for i in which:
            loads[i].wait()

    me = lax.axis_index("elem") * n_blk + lax.axis_index("blk")

    def device(step):
        other = lax.rem(me + step + devices, devices)
        return (other // n_blk, lax.rem(other, n_blk))

    steps = [s for s in range(-REACH, REACH + 1) if s]
    barrier = pltpu.get_barrier_semaphore()
    for s in steps:
        pl.semaphore_signal(barrier, inc=1, device_id=device(s), device_id_type=MESH)

    def remote(src, dst, ssem, rsem, step):
        return pltpu.make_async_remote_copy(
            src_ref=src,
            dst_ref=dst,
            send_sem=ssem,
            recv_sem=rsem,
            device_id=device(step),
            device_id_type=MESH,
        )

    def z_trace(refs, top):
        at = 48 if top else 0
        return jnp.concatenate([r[o + at : o + at + 16, :] for r, o in refs], 0)

    fields = [(q_ref, 0), (q_ref, 64), (q_ref, 128), (q_ref, 192), (f_ref, 192)]
    need(6)
    for way in range(2):
        exps[way] = hot(ex_ref[way : way + 1, :], 512)
    need(0, 1, 4)
    psend[...] = jnp.broadcast_to(ps_ref[...], psend.shape)
    for way in range(2):
        both = stack(z_trace(fields, way == 0))
        x2[way * 160 : way * 160 + 160, :] = both
        gathered = dot(both, exps[way])
        send1[way] = gathered[:80] + gathered[80:]
    pl.semaphore_wait(barrier, len(steps))
    copies1 = []
    for way in range(2):
        copy = remote(send1.at[way], recv1.at[way], ssem1.at[way], rsem1.at[way], 1 - 2 * way)
        copy.start()
        copies1.append(copy)
    pcopies = []
    for i, s in enumerate(steps):
        copy = remote(psend, table.at[REACH - s], pssem.at[i], prsem.at[REACH - s], s)
        copy.start()
        pcopies.append(copy)

    for i in LATE:
        loads[i].start()

    need(5)
    for f in range(6):
        hots[f] = hot(nb_ref[f : f + 1, :], 512)
    for way in range(2):
        ghots[way] = hot(nb_ref[4 + way : 5 + way, :], 256, 512)
    q_h, q_l = split(q_ref[...])
    x1[0:256, :] = q_h
    x1[256:512, :] = q_l
    u_h, u_l = split(f_ref[64:256, :])
    xs[0:192, :] = u_h
    xs[192:384, :] = u_l
    for way in range(2):
        inside = dot(x2[way * 160 : way * 160 + 160, :], hots[4 + way])
        wz[way] = inside[:80] + inside[80:]
    need(14, 15)
    t_h = dot(sel_t[...], x1[0:256, :]).astype(BF16)
    t_l = dot(sel_t[...], x1[256:512, :]).astype(BF16)
    tf_h = dot(sel_f[...], xs[0:128, :]).astype(BF16)
    tf_l = dot(sel_f[...], xs[192:320, :]).astype(BF16)
    for f in range(4):
        big = slice(64 * f, 64 * f + 64)
        small = slice(16 * f, 16 * f + 16)
        lhs = jnp.concatenate([t_h[big], t_l[big], tf_h[small], tf_l[small]], 0)
        far = dot(lhs, hots[f]).astype(BF16)
        x1[512 + 64 * f : 576 + 64 * f, :] = far[0:64]
        x1[768 + 64 * f : 832 + 64 * f, :] = far[64:128]
        xs[384 + 16 * f : 400 + 16 * f, :] = far[128:144]
        xs[448 + 16 * f : 464 + 16 * f, :] = far[144:160]
    need(8, 9, 10, 11, 3, 7)
    main = dot(main_m[...], x1[...])
    main_low = dot(main_l[...], x1[0:256, :])
    sense = dot(sens_m[...], xs[...]) + dot(sens_l[...], xs[0:192, :])
    bulk = jnp.broadcast_to(k_ref[...], (64, 512))

    pm = pm_ref[...]
    cells = ps_ref.shape[1]
    owner = pm // cells
    cell = pm - owner * cells
    where = owner - me + REACH
    where = jnp.where(where < 0, where + devices, where)
    where = jnp.where(where >= devices, where - devices, where)
    cell_hot = hot(cell, cells)
    blocks = pm.shape[1]
    repeat = jnp.where(
        lax.broadcasted_iota(jnp.int32, (blocks, 512), 1) // BLOCK
        == lax.broadcasted_iota(jnp.int32, (blocks, 512), 0),
        1.0,
        0.0,
    ).astype(BF16)
    for copy in pcopies:
        copy.wait()
    table[REACH] = psend[...]
    span = 2 * REACH + 1
    picked = dot(stack(table[...].reshape(8 * span, cells)), cell_hot)
    picked = picked[: 8 * span] + picked[8 * span :]
    block_step = jnp.zeros((8, blocks), F32)
    for o in range(span):
        block_step = jnp.where(where == o, picked[8 * o : 8 * o + 8], block_step)
    spread = dot(stack(block_step), repeat)
    step = jnp.concatenate([spread[:8] + spread[8:]] * 8, 0)

    need(17, 2)

    def advance(first, last, face=None):
        count = wide(count_ref[first:last, :])
        size = last - first
        s_part = sense[first:last]
        r_a = main[first:last]
        r_b = main[64 + first : 64 + last] + main_low[first:last]
        if face is not None:
            sign, far = face
            s_part = s_part - HALF * sign * far[64:80]
            r_a = r_a + HALF * far[0:16]
            r_b = r_b - HALF * sign * far[48:64]
        r_b = r_b + 2.0 * step[0:size] * s_part
        q = q_ref[first:last, :]
        new = q - count * q + DT * (r_a + bulk[0:size] * r_b)
        t_out[first:last, :] = new
        lam_p = a_ref[first:last, :] + new
        k_lam = bulk[0:size] * lam_p
        a_out[first:last, :] = lam_p
        states = [k_lam]
        for k in range(3):
            low, high = 64 + 64 * k + first, 64 + 64 * k + last
            r_u = main[64 + low : 64 + high] + main_low[low:high]
            if face is not None:
                add = far[16 + 16 * k : 32 + 16 * k]
                if k == 2:
                    add = add - sign * far[0:16]
                r_u = r_u + HALF * add
            q = q_ref[low:high, :]
            new = q - count * q + DT * r_u
            t_out[low:high, :] = new
            lam = a_ref[low:high, :] + new
            a_out[low:high, :] = lam
            states.append(lam)
        states.append(lam_p)
        return states, s_part

    def keep(states, first, last):
        for i, value in enumerate(states):
            high, low = split(value)
            x2[64 * i + first : 64 * i + last, :] = high
            x2[320 + 64 * i + first : 320 + 64 * i + last, :] = low

    copies2 = []
    zboth = []
    ends = []
    for way in range(2):
        copies1[way].wait()
        outside = dot(stack(recv1[way]), ghots[way])
        far = wz[way] + outside[:80] + outside[80:]
        at = 48 * way
        states, s_part = advance(at, at + 16, (2.0 * way - 1.0, far))
        both = stack(jnp.concatenate(states, 0))
        gathered = dot(both, exps[1 - way])
        send2[way] = gathered[:80] + gathered[80:]
        copy = remote(send2.at[way], recv2.at[way], ssem2.at[way], rsem2.at[way], 2 * way - 1)
        copy.start()
        copies2.append(copy)
        zboth.append(both)
        ends.append((states, s_part))
    middle = advance(16, 48)
    for way in range(2):
        keep(ends[way][0], 48 * way, 48 * way + 16)
    keep(middle[0], 16, 48)
    lam_p = jnp.concatenate([ends[0][0][4], middle[0][4], ends[1][0][4]], 0)
    sense = jnp.concatenate([ends[0][1], middle[1], ends[1][1]], 0)

    def z_add(value, first, last):
        return jnp.concatenate([value[0:16] + first, value[16:48], value[48:64] + last], 0)

    count = wide(count_ref[...])

    need(18)
    term = bulk * wide(mass_ref[...]) * lam_p * sense
    total = term[0:8]
    for i in range(1, 8):
        total = total + term[8 * i : 8 * i + 8]
    block_term = dot_nt(stack(total), repeat)
    block_term = block_term[:8] + block_term[8:]
    parts = jnp.concatenate([jnp.where(where == o, block_term, 0.0) for o in range(span)], 0)
    owned = dot_nt(stack(parts), cell_hot)
    owned = owned[: 8 * span] + owned[8 * span :]
    hsend[...] = owned.reshape(span, 8, cells)
    hcopies = []
    for i, s in enumerate(steps):
        copy = remote(hsend.at[REACH + s], hrecv.at[i], hssem.at[i], hrsem.at[i], s)
        copy.start()
        hcopies.append(copy)

    need(16, 12, 13)
    for way in range(2):
        inside = dot(zboth[1 - way], hots[4 + way])
        wz[way] = inside[:80] + inside[80:]
    t_h = dot(sel_a[...], x2[0:320, :]).astype(BF16)
    t_l = dot(sel_a[...], x2[320:640, :]).astype(BF16)
    x2[256:512, :] = x2[320:576, :]
    for f in range(4):
        rows = slice(80 * f, 80 * f + 80)
        far = dot(jnp.concatenate([t_h[rows], t_l[rows]], 0), hots[f]).astype(BF16)
        x2[512 + 80 * f : 592 + 80 * f, :] = far[0:80]
        x2[832 + 80 * f : 912 + 80 * f, :] = far[80:160]
    result = dot(adj_m[...], x2[...]) + dot(adj_l[...], x2[0:256, :])

    for way in range(2):
        copies2[way].wait()
        outside = dot(stack(recv2[way]), ghots[1 - way])
        wz[1 - way] = wz[1 - way] + outside[:80] + outside[80:]
    low, high = wz[0], wz[1]
    for k in range(4):
        at = 64 * k
        if k == 0:
            first = low[64:80] - low[48:64]
            last = high[64:80] + high[48:64]
        else:
            first, last = low[16 * k : 16 * k + 16], high[16 * k : 16 * k + 16]
            if k == 3:
                first = first - low[0:16]
                last = last + high[0:16]
        r = z_add(result[at : at + 64], HALF * first, HALF * last)
        lam = a_out[at : at + 64, :]
        a_out[at : at + 64, :] = lam - count * lam + DT * r

    for copy in hcopies:
        copy.wait()
    total = hsend[REACH]
    for i in range(len(steps)):
        total = total + hrecv[i]
    h_out[...] = jnp.sum(total, 0, keepdims=True)


def place(t_ref, a_ref, h_ref, t_out, a_out, h_out, t_mid, a_mid, h_mid, isem, osem):
    ways = ((t_ref, t_mid, t_out), (a_ref, a_mid, a_out), (h_ref, h_mid, h_out))
    ins = [pltpu.make_async_copy(w[0], w[1], isem.at[i]) for i, w in enumerate(ways)]
    outs = [pltpu.make_async_copy(w[1], w[2], osem.at[i]) for i, w in enumerate(ways)]
    for copy in ins:
        copy.start()
    for arrived, copy in zip(ins, outs):
        arrived.wait()
        copy.start()
    for copy in outs:
        copy.wait()


def solution(mesh):
    axes = ("elem", "blk")
    devices = mesh.shape["elem"] * mesh.shape["blk"]
    n_blk = mesh.shape["blk"]
    consts = tables()

    def local(tangent, forward, adjoint, bulk, param, neighbours, exports, param_map):
        hbm = pl.BlockSpec(memory_space=pltpu.HBM)
        vmem = pl.BlockSpec(memory_space=pltpu.VMEM)
        args = [
            tangent.reshape(256, 512),
            forward.reshape(256, 512),
            adjoint.reshape(256, 512),
            bulk.reshape(1, 512),
            param.reshape(1, -1),
            neighbours,
            exports,
            param_map.reshape(1, -1),
            *[jnp.asarray(c) for c in consts],
        ]
        span = 2 * REACH + 1
        cells = param.shape[0]
        dma = pltpu.SemaphoreType.DMA
        t_out, a_out, h_out = pl.pallas_call(
            functools.partial(kernel, devices, n_blk),
            out_shape=(
                jax.ShapeDtypeStruct((256, 512), F32),
                jax.ShapeDtypeStruct((256, 512), F32),
                jax.ShapeDtypeStruct((1, cells), F32),
            ),
            in_specs=[hbm] * INPUTS,
            out_specs=(vmem,) * 3,
            scratch_shapes=[pltpu.VMEM(a.shape, a.dtype) for a in args]
            + [
                dma((INPUTS,)),
                pltpu.VMEM((6, 512, 512), BF16),
                pltpu.VMEM((2, 256, 512), BF16),
                pltpu.VMEM((2, 512, 256), BF16),
                pltpu.VMEM((1024, 512), BF16),
                pltpu.VMEM((512, 512), BF16),
                pltpu.VMEM((1152, 512), BF16),
                pltpu.VMEM((2, 80, 512), F32),
                pltpu.VMEM((2, 80, 256), F32),
                pltpu.VMEM((2, 80, 256), F32),
                pltpu.VMEM((2, 80, 256), F32),
                pltpu.VMEM((2, 80, 256), F32),
                pltpu.VMEM((span, 8, cells), F32),
                pltpu.VMEM((8, cells), F32),
                pltpu.VMEM((span, 8, cells), F32),
                pltpu.VMEM((2 * REACH, 8, cells), F32),
                dma((2,)),
                dma((2,)),
                dma((2,)),
                dma((2,)),
                dma((2 * REACH,)),
                dma((span,)),
                dma((2 * REACH,)),
                dma((2 * REACH,)),
            ],
            compiler_params=pltpu.CompilerParams(
                collective_id=0, has_side_effects=True, vmem_limit_bytes=62 * 2**20
            ),
        )(*args)
        outs = (t_out, a_out, h_out)
        any_space = pl.BlockSpec(memory_space=pl.ANY)
        t_out, a_out, h_out = pl.pallas_call(
            place,
            out_shape=tuple(jax.ShapeDtypeStruct(o.shape, o.dtype) for o in outs),
            in_specs=[any_space] * 3,
            out_specs=(any_space,) * 3,
            scratch_shapes=[pltpu.VMEM(o.shape, o.dtype) for o in outs] + [dma((3,)), dma((3,))],
        )(*outs)
        return (
            t_out.reshape(4, 64, 512),
            a_out.reshape(4, 64, 512),
            h_out.reshape(cells),
        )

    whole = P(None, None, axes)
    row = P(axes)
    return jax.shard_map(
        local,
        mesh=mesh,
        in_specs=(whole, whole, whole, row, row, P(None, axes), P(None, axes), row),
        out_specs=(whole, whole, row),
        check_vma=False,
    )
```

```python
import functools

import jax
import jax.numpy as jnp
import ml_dtypes
import numpy as np
from jax import lax
from jax.experimental import pallas as pl
from jax.experimental.pallas import tpu as pltpu
from jax.sharding import PartitionSpec as P

BLOCK = 4
REACH = 2
LIFT = 6.0
DT = 0.1
HALF = 0.5 * LIFT
INPUTS = 19
EARLY = (6, 0, 1, 4, 5)
LATE = (14, 15, 8, 9, 10, 11, 7, 3, 17, 2, 18, 16, 12, 13)
MESH = pl.DeviceIdType.MESH
BF16 = jnp.bfloat16
F32 = jnp.float32


def split_np(matrix):
    high = matrix.astype(np.float32).astype(ml_dtypes.bfloat16)
    low = (matrix - high.astype(np.float64)).astype(np.float32).astype(ml_dtypes.bfloat16)
    return high, low


def tables():
    points = np.array([-1.0, -1.0 / np.sqrt(5.0), 1.0 / np.sqrt(5.0), 1.0])
    one = np.zeros((4, 4))
    for i in range(4):
        for j in range(4):
            if i != j:
                top = np.prod([points[i] - points[k] for k in range(4) if k != i and k != j])
                one[i, j] = top / np.prod([points[j] - points[k] for k in range(4) if k != j])
        one[i, i] = np.sum([1.0 / (points[i] - points[k]) for k in range(4) if k != i])
    eye = np.eye(4)
    deriv = [
        np.kron(np.eye(16), one),
        np.kron(eye, np.kron(one, eye)),
        np.kron(one, np.eye(16)),
    ]
    node = np.arange(64)
    place = [node % 4, node // 4 % 4, node // 16]
    faces = [np.flatnonzero(place[f // 2] == 3 * (f % 2)) for f in range(6)]
    sel = np.zeros((6, 16, 64))
    for f in range(6):
        sel[f, np.arange(16), faces[f]] = 1.0
    count = sel.sum((0, 1))
    local = []
    for d in range(3):
        ends = np.diag(sel[2 * d + 1].sum(0) - sel[2 * d].sum(0))
        local.append(-deriv[d] + HALF * ends)
    weights = np.array([1.0 / 6.0, 5.0 / 6.0, 5.0 / 6.0, 1.0 / 6.0])
    mass = np.kron(weights, np.kron(weights, weights))

    own = np.zeros((256, 256))
    for d in range(3):
        rows = slice(64 + 64 * d, 128 + 64 * d)
        own[:64, rows] = local[d]
        own[rows, :64] = local[d]
    sens = np.concatenate(local, 1)

    sel_t = np.zeros((256, 256))
    sel_f = np.zeros((64, 128))
    sel_a = np.zeros((320, 320))
    lift_t = np.zeros((320, 256))
    lift_s = np.zeros((64, 64))
    lift_a = np.zeros((256, 320))
    for f in range(4):
        d = f // 2
        s = 2.0 * (f % 2) - 1.0
        far = sel[f ^ 1]
        near = sel[f].T
        for k in range(4):
            sel_t[64 * f + 16 * k : 64 * f + 16 * k + 16, 64 * k : 64 * k + 64] = far
        for k in range(5):
            sel_a[80 * f + 16 * k : 80 * f + 16 * k + 16, 64 * k : 64 * k + 64] = far
        sel_f[16 * f : 16 * f + 16, 64 * d : 64 * d + 64] = far
        lift_s[:, 16 * f : 16 * f + 16] = -HALF * s * near
        at = 64 * f
        lift_t[0:64, at : at + 16] += HALF * near
        lift_t[64:128, at + 16 + 16 * d : at + 32 + 16 * d] += -HALF * s * near
        for k in range(3):
            lift_t[128 + 64 * k : 192 + 64 * k, at + 16 + 16 * k : at + 32 + 16 * k] += HALF * near
        lift_t[128 + 64 * d : 192 + 64 * d, at : at + 16] += -HALF * s * near
        at = 80 * f
        lift_a[0:64, at + 64 : at + 80] += HALF * near
        lift_a[0:64, at + 16 + 16 * d : at + 32 + 16 * d] += HALF * s * near
        for k in range(3):
            lift_a[64 + 64 * k : 128 + 64 * k, at + 16 + 16 * k : at + 32 + 16 * k] += HALF * near
        lift_a[64 + 64 * d : 128 + 64 * d, at : at + 16] += HALF * s * near

    own_h, own_l = split_np(own)
    adj_h, adj_l = split_np(own.T)
    sen_h, sen_l = split_np(sens)
    wide = np.zeros((320, 256), own_h.dtype)
    wide[64:] = own_h
    lift_t = lift_t.astype(own_h.dtype)
    lift_s = lift_s.astype(own_h.dtype)
    lift_a = lift_a.astype(own_h.dtype)
    return [
        np.concatenate([wide, wide, lift_t, lift_t], 1),
        own_l,
        np.concatenate([sen_h, sen_h, lift_s, lift_s], 1),
        sen_l,
        np.concatenate([adj_h, adj_h, lift_a, lift_a], 1),
        adj_l,
        sel_t.astype(own_h.dtype),
        sel_f.astype(own_h.dtype),
        sel_a.astype(own_h.dtype),
        np.repeat((DT * HALF * count)[:, None], 128, 1).astype(np.float32),
        np.repeat((2.0 * DT * mass)[:, None], 128, 1).astype(np.float32),
    ]


def dot(a, b):
    return jnp.dot(a, b, preferred_element_type=F32)


def dot_nt(a, b):
    return lax.dot_general(a, b, (((1,), (1,)), ((), ())), preferred_element_type=F32)


def split(value):
    high = value.astype(BF16)
    return high, (value - high.astype(F32)).astype(BF16)


def stack(value):
    return jnp.concatenate(split(value), 0)


def hot(row, rows, base=0):
    width = row.shape[1]
    at = lax.broadcasted_iota(jnp.int32, (rows, width), 0) + base
    return jnp.where(at == row, 1.0, 0.0).astype(BF16)


def wide(column):
    return jnp.concatenate([column] * 4, 1)


def kernel(
    devices,
    n_blk,
    *refs,
):
    sources, refs = refs[:INPUTS], refs[INPUTS:]
    t_hbm, a_out, h_out = refs[:3]
    refs = refs[3:]
    held, refs = refs[:INPUTS], refs[INPUTS:]
    (
    t_out,
    isem,
    osem,
    hots,
    ghots,
    exps,
    x1,
    xs,
    x2,
    wz,
    send1,
    recv1,
    send2,
    recv2,
    table,
    psend,
    hsend,
    hrecv,
    ssem1,
    rsem1,
    ssem2,
    rsem2,
    pssem,
    prsem,
    hssem,
    hrsem,
    ) = refs
    (
        q_ref,
        f_ref,
        a_ref,
        k_ref,
        ps_ref,
        nb_ref,
        ex_ref,
        pm_ref,
        main_m,
        main_l,
        sens_m,
        sens_l,
        adj_m,
        adj_l,
        sel_t,
        sel_f,
        sel_a,
        count_ref,
        mass_ref,
    ) = held
    loads = [
        pltpu.make_async_copy(sources[i], held[i], isem.at[i]) for i in range(INPUTS)
    ]
    for i in EARLY:
        loads[i].start()

    def need(*which):
        for i in which:
            loads[i].wait()

    me = lax.axis_index("elem") * n_blk + lax.axis_index("blk")

    def device(step):
        other = lax.rem(me + step + devices, devices)
        return (other // n_blk, lax.rem(other, n_blk))

    steps = [s for s in range(-REACH, REACH + 1) if s]
    barrier = pltpu.get_barrier_semaphore()
    for s in steps:
        pl.semaphore_signal(barrier, inc=1, device_id=device(s), device_id_type=MESH)

    def remote(src, dst, ssem, rsem, step):
        return pltpu.make_async_remote_copy(
            src_ref=src,
            dst_ref=dst,
            send_sem=ssem,
            recv_sem=rsem,
            device_id=device(step),
            device_id_type=MESH,
        )

    def z_trace(refs, top):
        at = 48 if top else 0
        return jnp.concatenate([r[o + at : o + at + 16, :] for r, o in refs], 0)

    fields = [(q_ref, 0), (q_ref, 64), (q_ref, 128), (q_ref, 192), (f_ref, 192)]
    need(6)
    for way in range(2):
        exps[way] = hot(ex_ref[way : way + 1, :], 512)
    need(0, 1, 4)
    psend[...] = jnp.broadcast_to(ps_ref[...], psend.shape)
    for way in range(2):
        both = stack(z_trace(fields, way == 0))
        x2[way * 160 : way * 160 + 160, :] = both
        gathered = dot(both, exps[way])
        send1[way] = gathered[:80] + gathered[80:]
    pl.semaphore_wait(barrier, len(steps))
    copies1 = []
    for way in range(2):
        copy = remote(send1.at[way], recv1.at[way], ssem1.at[way], rsem1.at[way], 1 - 2 * way)
        copy.start()
        copies1.append(copy)
    pcopies = []
    for i, s in enumerate(steps):
        copy = remote(psend, table.at[REACH - s], pssem.at[i], prsem.at[REACH - s], s)
        copy.start()
        pcopies.append(copy)

    for i in LATE:
        loads[i].start()

    need(5)
    for f in range(6):
        hots[f] = hot(nb_ref[f : f + 1, :], 512)
    for way in range(2):
        ghots[way] = hot(nb_ref[4 + way : 5 + way, :], 256, 512)
    q_h, q_l = split(q_ref[...])
    x1[0:256, :] = q_h
    x1[256:512, :] = q_l
    u_h, u_l = split(f_ref[64:256, :])
    xs[0:192, :] = u_h
    xs[192:384, :] = u_l
    for way in range(2):
        inside = dot(x2[way * 160 : way * 160 + 160, :], hots[4 + way])
        wz[way] = inside[:80] + inside[80:]
    need(14, 15)
    t_h = dot(sel_t[...], x1[0:256, :]).astype(BF16)
    t_l = dot(sel_t[...], x1[256:512, :]).astype(BF16)
    tf_h = dot(sel_f[...], xs[0:128, :]).astype(BF16)
    tf_l = dot(sel_f[...], xs[192:320, :]).astype(BF16)
    for f in range(4):
        big = slice(64 * f, 64 * f + 64)
        small = slice(16 * f, 16 * f + 16)
        lhs = jnp.concatenate([t_h[big], t_l[big], tf_h[small], tf_l[small]], 0)
        far = dot(lhs, hots[f]).astype(BF16)
        x1[512 + 64 * f : 576 + 64 * f, :] = far[0:64]
        x1[768 + 64 * f : 832 + 64 * f, :] = far[64:128]
        xs[384 + 16 * f : 400 + 16 * f, :] = far[128:144]
        xs[448 + 16 * f : 464 + 16 * f, :] = far[144:160]
    need(8, 9, 10, 11, 3, 7)
    main = dot(main_m[...], x1[...])
    main_low = dot(main_l[...], x1[0:256, :])
    sense = dot(sens_m[...], xs[...]) + dot(sens_l[...], xs[0:192, :])
    bulk = jnp.broadcast_to(k_ref[...], (64, 512))

    pm = pm_ref[...]
    cells = ps_ref.shape[1]
    owner = pm // cells
    cell = pm - owner * cells
    where = owner - me + REACH
    where = jnp.where(where < 0, where + devices, where)
    where = jnp.where(where >= devices, where - devices, where)
    cell_hot = hot(cell, cells)
    blocks = pm.shape[1]
    repeat = jnp.where(
        lax.broadcasted_iota(jnp.int32, (blocks, 512), 1) // BLOCK
        == lax.broadcasted_iota(jnp.int32, (blocks, 512), 0),
        1.0,
        0.0,
    ).astype(BF16)
    for copy in pcopies:
        copy.wait()
    table[REACH] = psend[...]
    span = 2 * REACH + 1
    picked = dot(stack(table[...].reshape(8 * span, cells)), cell_hot)
    picked = picked[: 8 * span] + picked[8 * span :]
    block_step = jnp.zeros((8, blocks), F32)
    for o in range(span):
        block_step = jnp.where(where == o, picked[8 * o : 8 * o + 8], block_step)
    spread = dot(stack(block_step), repeat)
    step = jnp.concatenate([spread[:8] + spread[8:]] * 8, 0)

    need(17, 2)

    def advance(first, last, face=None):
        count = wide(count_ref[first:last, :])
        size = last - first
        s_part = sense[first:last]
        r_a = main[first:last]
        r_b = main[64 + first : 64 + last] + main_low[first:last]
        if face is not None:
            sign, far = face
            s_part = s_part - HALF * sign * far[64:80]
            r_a = r_a + HALF * far[0:16]
            r_b = r_b - HALF * sign * far[48:64]
        r_b = r_b + 2.0 * step[0:size] * s_part
        q = q_ref[first:last, :]
        new = q - count * q + DT * (r_a + bulk[0:size] * r_b)
        t_out[first:last, :] = new
        lam_p = a_ref[first:last, :] + new
        k_lam = bulk[0:size] * lam_p
        a_out[first:last, :] = lam_p
        states = [k_lam]
        for k in range(3):
            low, high = 64 + 64 * k + first, 64 + 64 * k + last
            r_u = main[64 + low : 64 + high] + main_low[low:high]
            if face is not None:
                add = far[16 + 16 * k : 32 + 16 * k]
                if k == 2:
                    add = add - sign * far[0:16]
                r_u = r_u + HALF * add
            q = q_ref[low:high, :]
            new = q - count * q + DT * r_u
            t_out[low:high, :] = new
            lam = a_ref[low:high, :] + new
            a_out[low:high, :] = lam
            states.append(lam)
        states.append(lam_p)
        return states, s_part

    def keep(states, first, last):
        for i, value in enumerate(states):
            high, low = split(value)
            x2[64 * i + first : 64 * i + last, :] = high
            x2[320 + 64 * i + first : 320 + 64 * i + last, :] = low

    copies2 = []
    zboth = []
    ends = []
    for way in range(2):
        copies1[way].wait()
        outside = dot(stack(recv1[way]), ghots[way])
        far = wz[way] + outside[:80] + outside[80:]
        at = 48 * way
        states, s_part = advance(at, at + 16, (2.0 * way - 1.0, far))
        both = stack(jnp.concatenate(states, 0))
        gathered = dot(both, exps[1 - way])
        send2[way] = gathered[:80] + gathered[80:]
        copy = remote(send2.at[way], recv2.at[way], ssem2.at[way], rsem2.at[way], 2 * way - 1)
        copy.start()
        copies2.append(copy)
        zboth.append(both)
        ends.append((states, s_part))
    middle = advance(16, 48)
    leave = pltpu.make_async_copy(t_out, t_hbm, osem)
    leave.start()
    for way in range(2):
        keep(ends[way][0], 48 * way, 48 * way + 16)
    keep(middle[0], 16, 48)
    lam_p = jnp.concatenate([ends[0][0][4], middle[0][4], ends[1][0][4]], 0)
    sense = jnp.concatenate([ends[0][1], middle[1], ends[1][1]], 0)

    def z_add(value, first, last):
        return jnp.concatenate([value[0:16] + first, value[16:48], value[48:64] + last], 0)

    count = wide(count_ref[...])

    need(18)
    term = bulk * wide(mass_ref[...]) * lam_p * sense
    total = term[0:8]
    for i in range(1, 8):
        total = total + term[8 * i : 8 * i + 8]
    block_term = dot_nt(stack(total), repeat)
    block_term = block_term[:8] + block_term[8:]
    parts = jnp.concatenate([jnp.where(where == o, block_term, 0.0) for o in range(span)], 0)
    owned = dot_nt(stack(parts), cell_hot)
    owned = owned[: 8 * span] + owned[8 * span :]
    hsend[...] = owned.reshape(span, 8, cells)
    hcopies = []
    for i, s in enumerate(steps):
        copy = remote(hsend.at[REACH + s], hrecv.at[i], hssem.at[i], hrsem.at[i], s)
        copy.start()
        hcopies.append(copy)

    need(16, 12, 13)
    for way in range(2):
        inside = dot(zboth[1 - way], hots[4 + way])
        wz[way] = inside[:80] + inside[80:]
    t_h = dot(sel_a[...], x2[0:320, :]).astype(BF16)
    t_l = dot(sel_a[...], x2[320:640, :]).astype(BF16)
    x2[256:512, :] = x2[320:576, :]
    for f in range(4):
        rows = slice(80 * f, 80 * f + 80)
        far = dot(jnp.concatenate([t_h[rows], t_l[rows]], 0), hots[f]).astype(BF16)
        x2[512 + 80 * f : 592 + 80 * f, :] = far[0:80]
        x2[832 + 80 * f : 912 + 80 * f, :] = far[80:160]
    result = dot(adj_m[...], x2[...]) + dot(adj_l[...], x2[0:256, :])

    for way in range(2):
        copies2[way].wait()
        outside = dot(stack(recv2[way]), ghots[1 - way])
        wz[1 - way] = wz[1 - way] + outside[:80] + outside[80:]
    low, high = wz[0], wz[1]
    for k in range(4):
        at = 64 * k
        if k == 0:
            first = low[64:80] - low[48:64]
            last = high[64:80] + high[48:64]
        else:
            first, last = low[16 * k : 16 * k + 16], high[16 * k : 16 * k + 16]
            if k == 3:
                first = first - low[0:16]
                last = last + high[0:16]
        r = z_add(result[at : at + 64], HALF * first, HALF * last)
        lam = a_out[at : at + 64, :]
        a_out[at : at + 64, :] = lam - count * lam + DT * r

    for copy in hcopies:
        copy.wait()
    total = hsend[REACH]
    for i in range(len(steps)):
        total = total + hrecv[i]
    h_out[...] = jnp.sum(total, 0, keepdims=True)
    leave.wait()


def place(t_ref, a_ref, h_ref, t_out, a_out, h_out, t_mid, a_mid, h_mid, isem, osem):
    ways = ((t_ref, t_mid, t_out), (a_ref, a_mid, a_out), (h_ref, h_mid, h_out))
    ins = [pltpu.make_async_copy(w[0], w[1], isem.at[i]) for i, w in enumerate(ways)]
    outs = [pltpu.make_async_copy(w[1], w[2], osem.at[i]) for i, w in enumerate(ways)]
    for copy in ins:
        copy.start()
    for arrived, copy in zip(ins, outs):
        arrived.wait()
        copy.start()
    for copy in outs:
        copy.wait()


def solution(mesh):
    axes = ("elem", "blk")
    devices = mesh.shape["elem"] * mesh.shape["blk"]
    n_blk = mesh.shape["blk"]
    consts = tables()

    def local(tangent, forward, adjoint, bulk, param, neighbours, exports, param_map):
        hbm = pl.BlockSpec(memory_space=pltpu.HBM)
        vmem = pl.BlockSpec(memory_space=pltpu.VMEM)
        args = [
            tangent.reshape(256, 512),
            forward.reshape(256, 512),
            adjoint.reshape(256, 512),
            bulk.reshape(1, 512),
            param.reshape(1, -1),
            neighbours,
            exports,
            param_map.reshape(1, -1),
            *[jnp.asarray(c) for c in consts],
        ]
        span = 2 * REACH + 1
        cells = param.shape[0]
        dma = pltpu.SemaphoreType.DMA
        t_out, a_out, h_out = pl.pallas_call(
            functools.partial(kernel, devices, n_blk),
            out_shape=(
                jax.ShapeDtypeStruct((256, 512), F32),
                jax.ShapeDtypeStruct((256, 512), F32),
                jax.ShapeDtypeStruct((1, cells), F32),
            ),
            in_specs=[hbm] * INPUTS,
            out_specs=(hbm, vmem, vmem),
            scratch_shapes=[pltpu.VMEM(a.shape, a.dtype) for a in args]
            + [
                pltpu.VMEM((256, 512), F32),
                dma((INPUTS,)),
                dma(()),
                pltpu.VMEM((6, 512, 512), BF16),
                pltpu.VMEM((2, 256, 512), BF16),
                pltpu.VMEM((2, 512, 256), BF16),
                pltpu.VMEM((1024, 512), BF16),
                pltpu.VMEM((512, 512), BF16),
                pltpu.VMEM((1152, 512), BF16),
                pltpu.VMEM((2, 80, 512), F32),
                pltpu.VMEM((2, 80, 256), F32),
                pltpu.VMEM((2, 80, 256), F32),
                pltpu.VMEM((2, 80, 256), F32),
                pltpu.VMEM((2, 80, 256), F32),
                pltpu.VMEM((span, 8, cells), F32),
                pltpu.VMEM((8, cells), F32),
                pltpu.VMEM((span, 8, cells), F32),
                pltpu.VMEM((2 * REACH, 8, cells), F32),
                dma((2,)),
                dma((2,)),
                dma((2,)),
                dma((2,)),
                dma((2 * REACH,)),
                dma((span,)),
                dma((2 * REACH,)),
                dma((2 * REACH,)),
            ],
            compiler_params=pltpu.CompilerParams(
                collective_id=0, has_side_effects=True, vmem_limit_bytes=62 * 2**20
            ),
        )(*args)
        outs = (t_out, a_out, h_out)
        any_space = pl.BlockSpec(memory_space=pl.ANY)
        t_out, a_out, h_out = pl.pallas_call(
            place,
            out_shape=tuple(jax.ShapeDtypeStruct(o.shape, o.dtype) for o in outs),
            in_specs=[any_space] * 3,
            out_specs=(any_space,) * 3,
            scratch_shapes=[pltpu.VMEM(o.shape, o.dtype) for o in outs] + [dma((3,)), dma((3,))],
        )(*outs)
        return (
            t_out.reshape(4, 64, 512),
            a_out.reshape(4, 64, 512),
            h_out.reshape(cells),
        )

    whole = P(None, None, axes)
    row = P(axes)
    return jax.shard_map(
        local,
        mesh=mesh,
        in_specs=(whole, whole, whole, row, row, P(None, axes), P(None, axes), row),
        out_specs=(whole, whole, row),
        check_vma=False,
    )
```
